256 devices in a mesh: ctx: 16 (over y, x_hi, core), head: 16 (over x_lo, z).
Axes of the slice: x: 4 (x_hi: 2, x_lo: 2; x = x_hi * 2 + x_lo), y: 4, z: 8, core: 2. Of those that a mesh axis runs over, the one named last changes fastest.
Arguments:
- tokens: bfloat16 [16384, 2048], P('ctx', 'head'), may hold values from -6 to 6
- w_query: bfloat16 [2048, 2048], P(None, 'head'), may hold values from -0.125 to 0.125
- w_value: bfloat16 [2048, 2048], P(None, 'head'), may hold values from -0.125 to 0.125
- w_out: bfloat16 [2048, 2048], P('head'), may hold values from -1.5 to 1.5
- doc_lengths: int32 [2], replicated, may hold values from 1024 to 8192, as said below
Outputs:
- layer_out: bfloat16 [16384, 2048], P('ctx', 'head')
The draws below stay inside these ranges and needn't reach their ends.
Inputs may be any that keep to these rules, and one draw needn't show every extreme that they name: `doc_lengths`: one of the two documents, drawn from the seed, has the full length 8192; the other has at least 1024 valid tokens.
All inputs are finite; a program needn't handle non-finite values.
Results may differ from the reference program's by a relative error of at most 0.02.
Values may be sent and summed in bfloat16 or wider, within the bound.
No kernel may reach another device: no remote copies, remote signals or barrier semaphores. Data moves between devices by JAX's collectives and lax.ppermute only.
A program may use at most 64 MiB of HBM per device.

```python
import jax
import jax.numpy as jnp
from jax import lax

D = 2048
H = 16
HD = 128
TOK_DEV = 1024
DOC_LEN = 8192
TOKENS = 16384


def draw_lengths(key, part):
    lowest = max(DOC_LEN // 8, 2)
    picked = jax.random.randint(jax.random.fold_in(key, 11), (2,), lowest, DOC_LEN + 1)
    full_doc = jax.random.randint(jax.random.fold_in(key, 12), (), 0, 2)
    return jnp.where(jnp.arange(2) == full_doc, DOC_LEN, picked).astype(jnp.int32)


def draw_doc_lengths(key, part):
    return draw_lengths(key, part)


def with_spikes(entries, stream_key, source, target, blocks, factor):
    def block_of(dim):
        return (jnp.arange(entries.shape[dim]) // (entries.shape[dim] // blocks)).reshape((-1,) + (1,) * (entries.ndim - 1 - dim))

    near = jax.random.permutation(stream_key, blocks)[block_of(target)]
    far = (block_of(target) + blocks // 2) % blocks
    return jnp.where((block_of(source) == near) | (block_of(source) == far), factor * entries, entries)


def steps_of(key, extent, cuts, smallest, high):
    loudness, own = 1.0, jax.random.fold_in(key, 6)
    for dim, shards_of in cuts:
        draws = jnp.exp(jax.random.uniform(jax.random.fold_in(own, dim), (shards_of,), jnp.float32, smallest / len(cuts), high / len(cuts)))
        loudness = loudness * jnp.repeat(draws, extent[dim] // shards_of).reshape([-1 if axis == dim else 1 for axis in range(len(extent))])
    return loudness


def gaussian(rng, dims, spread, bound, shards=(), kind=jnp.bfloat16):
    values = jax.random.normal(rng, dims, jnp.float32) * spread
    if len(shards) > 0:
        values = steps_of(rng, dims, shards, -0.22, 0.18) * values
    return jnp.clip(values, min=-bound, max=bound).astype(kind)


def noise_with(rng, dims, width, reach, split, heavy, kind=jnp.bfloat16):
    entries = width * jax.random.normal(rng, dims, jnp.float32)
    if split:
        entries = entries * steps_of(rng, dims, split, -0.22, 0.18)
    return jnp.clip(with_spikes(entries, jax.random.fold_in(rng, 3), *heavy), -reach, reach).astype(kind)


def setup_inputs(seed: int = 0) -> dict:
    splits = jax.random.split(jax.random.key(seed), 6)
    tokens = gaussian(splits[0], (TOKENS, D), 1.0, 6.0, ((0, 16), (1, 16)))
    w_query = gaussian(splits[1], (D, H * HD), D ** -0.5, 0.125, ((1, 16),))
    w_value = gaussian(splits[2], (D, H * HD), D ** -0.5, 0.125, ((1, 16),))
    w_out = noise_with(splits[3], (H * HD, D), (HD // 4) ** -0.5, 1.5, ((0, 16),), (0, 1, 16, 2.0))
    doc_lengths = draw_doc_lengths(jax.random.fold_in(splits[5], 71), 0)
    return {"tokens": tokens, "w_query": w_query, "w_value": w_value, "w_out": w_out, "doc_lengths": doc_lengths}


score_bound = 24.0

def reference(tokens, w_query, w_value, w_out, doc_lengths):
    projected = jnp.dot(tokens, w_query, preferred_element_type=jnp.float32).reshape(TOKENS, H, HD)
    unit_rows = projected * lax.rsqrt(lax.optimization_barrier(jnp.sum(projected * projected, axis=-1, keepdims=True)) + 1e-06)
    unit_rows = lax.optimization_barrier(unit_rows.astype(jnp.bfloat16)).astype(jnp.float32)
    value_rows = jnp.dot(tokens, w_value, preferred_element_type=jnp.float32).astype(jnp.bfloat16)
    value_rows = lax.optimization_barrier(value_rows).astype(jnp.float32).reshape(TOKENS, H, HD)
    position = jnp.arange(TOKENS, dtype=jnp.int32)
    doc_index = position // DOC_LEN
    limit = jnp.where(doc_index == 0, doc_lengths[0], doc_lengths[1])
    valid_rows = (position - doc_index * DOC_LEN < limit).astype(jnp.float32)
    per_doc = DOC_LEN // TOK_DEV

    def one_block(block_index):
        start = (block_index * TOK_DEV).astype(jnp.int32)
        query_rows = lax.dynamic_slice_in_dim(unit_rows, start, TOK_DEV, 0)
        query_valid = lax.dynamic_slice_in_dim(valid_rows, start, TOK_DEV, 0)
        query_position = start + jnp.arange(TOK_DEV, dtype=jnp.int32)
        doc_start = (start // DOC_LEN * DOC_LEN).astype(jnp.int32)

        def add_keys(key_block, totals):
            numer, denom = totals
            key_start = (doc_start + key_block * TOK_DEV).astype(jnp.int32)
            key_rows = lax.dynamic_slice_in_dim(unit_rows, key_start, TOK_DEV, 0)
            key_values = lax.dynamic_slice_in_dim(value_rows, key_start, TOK_DEV, 0)
            key_valid = lax.dynamic_slice_in_dim(valid_rows, key_start, TOK_DEV, 0)
            key_position = key_start + jnp.arange(TOK_DEV, dtype=jnp.int32)
            distinct = (query_position[:, None] != key_position[None, :]).astype(jnp.float32)
            pair_mask = query_valid[:, None] * key_valid[None, :] * distinct
            scores = jnp.einsum('qhd,khd->hqk', query_rows, key_rows) * score_bound
            tile = jnp.exp(scores - score_bound) * pair_mask[None]
            denom = denom + lax.optimization_barrier(jnp.sum(tile, axis=2))
            rounded = lax.optimization_barrier(tile.astype(jnp.bfloat16)).astype(jnp.float32)
            numer = numer + jnp.einsum('hqk,khd->qhd', rounded, key_values)
            return (numer, denom)
        start_totals = (jnp.zeros((TOK_DEV, H, HD), jnp.float32), jnp.zeros((H, TOK_DEV), jnp.float32))
        numer, denom = lax.fori_loop(0, per_doc, add_keys, start_totals)
        attended = numer / (denom.T[:, :, None] + (1.0 - query_valid)[:, None, None])
        return attended.astype(jnp.bfloat16)
    blocks = lax.map(one_block, jnp.arange(TOKENS // TOK_DEV, dtype=jnp.int32))
    attended = blocks.reshape(TOKENS, H * HD)
    return jnp.dot(attended, w_out, preferred_element_type=jnp.float32).astype(jnp.bfloat16)
```

```python
import itertools
import math

import jax
import jax.numpy as jnp
from jax import lax
from jax.experimental import pallas as pl
from jax.experimental.pallas import tpu as pltpu
from jax.sharding import Mesh
from jax.sharding import PartitionSpec as P

HD = 128
HEAD = ("xl", "z")
CTX = ("yh", "yl", "xh", "core")
AXES = CTX + HEAD
SCORE_BOUND = 24.0
SCALE = SCORE_BOUND * math.log2(math.e)
VMEM = pl.BlockSpec(memory_space=pltpu.VMEM)
SMEM = pl.BlockSpec(memory_space=pltpu.SMEM)
F32 = jnp.float32
BF16 = jnp.bfloat16


def hop(value, axes, target):
    places = list(itertools.product(*(range(lax.axis_size(a)) for a in axes)))
    number = {place: i for i, place in enumerate(places)}
    return lax.ppermute(value, axes, [(number[c], number[tuple(target(*c))]) for c in places])


def swap(value, *axes):
    return hop(value, axes, lambda *c: tuple(1 - i for i in c))


def z_step(value):
    depth = lax.axis_size("z")
    return hop(value, ("core", "z"), lambda c, z: (c, (z + 1 - 2 * c) % depth))


def params(mib):
    return pltpu.CompilerParams(vmem_limit_bytes=mib * 2**20)


def call(kernel, outs, smem_count, args, name, flops, limit=24):
    moved = sum(math.prod(a.shape) * a.dtype.itemsize for a in [*args, *outs])
    return pl.pallas_call(
        kernel,
        out_shape=outs,
        in_specs=[SMEM] * smem_count + [VMEM] * (len(args) - smem_count),
        out_specs=[VMEM] * len(outs),
        compiler_params=params(limit),
        cost_estimate=pl.CostEstimate(flops=flops, bytes_accessed=moved, transcendentals=0),
        name=name,
    )(*args)


def contract(rows_at, weights, jobs, name, finish=None, extras=(), outs=None, smem=()):
    width = sum(w.shape[1] for w in weights)
    flat, plan = [], []
    for total, *terms in jobs:
        plan.append((total is not None, [t[0] for t in terms]))
        flat += ([total] if total is not None else []) + [b for t in terms for b in t[1:]]
    rows = jobs[0][1][1].shape[0]
    tile = 256
    if outs is None:
        outs = [jax.ShapeDtypeStruct((rows, width), F32)] * len(jobs)
    n_s, n_w, n_e, n_f = 1 + len(smem), len(weights), len(extras), len(flat)

    def kernel(*refs):
        at = refs[0]
        w_refs = refs[n_s : n_s + n_w]
        e_refs = refs[n_s + n_w : n_s + n_w + n_e]
        b_refs = list(refs[n_s + n_w + n_e : n_s + n_w + n_e + n_f])
        o_refs = refs[n_s + n_w + n_e + n_f :]
        taken = {}

        def weight(step):
            if step not in taken:
                halves = []
                for i in (0, 1):
                    first = pl.multiple_of(at[2 * step + i], HD)
                    halves.append(
                        jnp.concatenate([w[pl.ds(first, HD), :] for w in w_refs], axis=1)
                    )
                taken[step] = jnp.concatenate(halves, axis=0)
            return taken[step]

        for index, (has_total, steps) in enumerate(plan):
            total_ref = b_refs.pop(0) if has_total else None
            pairs = [(s, b_refs.pop(0), b_refs.pop(0)) for s in steps]
            for first in range(0, rows, tile):
                here = slice(first, first + tile)
                total = None if total_ref is None else total_ref[here, :]
                for s, one, two in pairs:
                    both = jnp.concatenate([one[here, :], two[here, :]], axis=1)
                    term = jnp.dot(both, weight(s), preferred_element_type=F32)
                    total = term if total is None else total + term
                if finish is None:
                    o_refs[index][here, :] = total.astype(o_refs[index].dtype)
                else:
                    finish(refs[1:n_s], e_refs, o_refs, total, first, tile)

    terms = sum(len(steps) for _, steps in plan)
    return call(
        kernel,
        outs,
        n_s,
        [rows_at, *smem, *weights, *extras, *flat],
        name,
        2 * rows * 256 * width * terms,
    )


def finish_units(smem, extras, outs, total, first, tile):
    here = slice(first, first + tile)
    total = total + extras[0][here, :]
    proj = total[:, :HD]
    unit = proj * lax.rsqrt(jnp.sum(proj * proj, axis=-1, keepdims=True) + 1e-06)
    row = lax.broadcasted_iota(jnp.int32, (tile, HD), 0) + first
    value = jnp.where(row < smem[0][0], total[:, HD:], 0.0).astype(BF16)
    unit = unit.astype(BF16)
    outs[0][here, :HD] = unit
    outs[0][here, HD:] = value
    outs[1][here, :] = unit


def finish_out(smem, extras, outs, total, first, tile):
    here = slice(first, first + tile)
    outs[0][here, :] = (total + extras[0][here, :]).astype(BF16)


def attend(limits, groups, blocks, name, out_type=F32, tile_q=512, tile_k=512):
    n_b = len(blocks)
    flat, plan = [], []
    for queries, total, own in groups:
        plan.append((total is not None, own))
        flat += [queries] + ([total] if total is not None else [])
    rows = groups[0][0].shape[0]
    outs = [jax.ShapeDtypeStruct((rows, 2 * HD), out_type)] * len(groups)

    def kernel(*refs):
        limit = refs[0]
        kv_refs = refs[1 : 1 + n_b]
        g_refs = list(refs[1 + n_b : 1 + n_b + len(flat)])
        o_refs = refs[1 + n_b + len(flat) :]
        for index, (has_total, own) in enumerate(plan):
            q_ref = g_refs.pop(0)
            t_ref = g_refs.pop(0) if has_total else None

            @pl.loop(0, rows // tile_q)
            def _(step):
                first = pl.multiple_of(step * tile_q, tile_q)
                here = pl.ds(first, tile_q)
                queries = q_ref[here, :]
                total = None if t_ref is None else t_ref[here, :]
                for b, kv in enumerate(kv_refs):
                    for start in range(0, kv.shape[0], tile_k):
                        keys = kv[start : start + tile_k, :HD]
                        values = kv[start : start + tile_k, HD:]
                        row = lax.broadcasted_iota(jnp.int32, (tile_k, HD), 0) + start
                        counted = jnp.where(row < limit[b], 1.0, 0.0).astype(BF16)
                        scores = lax.dot_general(
                            queries, keys, (((1,), (1,)), ((), ())), preferred_element_type=F32
                        )
                        weights = jnp.exp2(scores * SCALE - SCALE)
                        if own and b == 0:
                            q_at = lax.broadcasted_iota(jnp.int32, weights.shape, 0) + first
                            k_at = lax.broadcasted_iota(jnp.int32, weights.shape, 1) + start
                            weights = jnp.where(q_at == k_at, 0.0, weights)
                        term = jnp.dot(
                            weights.astype(BF16),
                            jnp.concatenate([values, counted], axis=1),
                            preferred_element_type=F32,
                        )
                        total = term if total is None else total + term
                o_refs[index][here, :] = total.astype(out_type)

    flops = len(groups) * n_b * 4 * rows * blocks[0].shape[0] * HD * 2
    return call(kernel, outs, 1, [limits, *blocks, *flat], name, flops)


def combine(limits, mine, theirs, name):
    rows = mine.shape[0]

    def kernel(limit, a_ref, b_ref, o_ref):
        total = a_ref[...] + b_ref[...].astype(F32)
        row = lax.broadcasted_iota(jnp.int32, (rows, HD), 0)
        valid = row < limit[0]
        denom = jnp.where(valid, total[:, HD:], 1.0)
        o_ref[...] = jnp.where(valid, total[:, :HD] / denom, 0.0).astype(BF16)

    out = jax.ShapeDtypeStruct((rows, HD), BF16)
    return call(kernel, [out], 1, [limits, mine, theirs], name, rows * HD * 8)[0]


def gathered_product(block, rows_at, weights, finish, outs, smem, name):
    depth = lax.axis_size("z")
    half = depth // 2
    own, cross = block, swap(block, "xl")
    other = swap(block, "core")
    mine = [(0, own, cross)]
    both = None
    total_own = total_other = None
    for s in range(1, half):
        own, other, cross = z_step(own), z_step(other), z_step(cross)
        mine.append((s, own, cross))
        far = (s, other, swap(other, "xl"))
        if s < half - 1:
            total_own, total_other = contract(
                rows_at, weights, [[total_own, *mine], [total_other, far]], f"{name}_{s}"
            )
            mine = []
        else:
            (total_other,) = contract(
                rows_at, weights, [[total_other, far]], f"{name}_{s}"
            )
            both = swap(total_other, "core")
    own, cross = z_step(own), z_step(cross)
    mine.append((half, own, cross))
    return contract(
        rows_at,
        weights,
        [[total_own, *mine]],
        f"{name}_last",
        finish=finish,
        extras=[both],
        outs=outs,
        smem=smem,
    )


def per_device(tokens, w_query, w_value, w_out, doc_lengths):
    rows = tokens.shape[0]
    depth = lax.axis_size("z")
    xl, z, core = lax.axis_index("xl"), lax.axis_index("z"), lax.axis_index("core")
    heads = lax.axis_size(HEAD)

    steps = jnp.arange(depth // 2 + 1, dtype=jnp.int32)
    z_at = (z + jnp.where(core == 0, -steps, steps)) % depth
    rows_at = (jnp.stack([xl * depth + z_at, (1 - xl) * depth + z_at], 1).reshape(-1) * HD).astype(
        jnp.int32
    )

    in_doc = (lax.axis_index("yl") * 2 + lax.axis_index("xh")) * 2 + core
    limit = doc_lengths[lax.axis_index("yh")]

    def limits(*masks):
        return jnp.stack([limit - (in_doc ^ m) * rows for m in masks]).astype(jnp.int32)

    w_cols = lax.all_to_all(
        jnp.moveaxis(w_out.reshape(HD, heads, HD), 1, 0), HEAD, 0, 0
    ).reshape(heads * HD, HD)

    joined, unit = gathered_product(
        tokens,
        rows_at,
        [w_query, w_value],
        finish_units,
        [jax.ShapeDtypeStruct((rows, 2 * HD), BF16), jax.ShapeDtypeStruct((rows, HD), BF16)],
        [limits(0)],
        "project",
    )
    unit_other = swap(unit, "core")
    from_y, from_x = swap(joined, "yl"), swap(joined, "xh")
    from_yx = swap(joined, "yl", "xh")

    own, other = attend(
        limits(0), [(unit, None, True), (unit_other, None, False)], [joined], "attend_own"
    )
    own, other = attend(
        limits(4, 2), [(unit, own, False), (unit_other, other, False)], [from_y, from_x], "attend_near"
    )
    (other,) = attend(
        limits(6), [(unit_other, other, False)], [from_yx], "attend_far_other", out_type=BF16
    )
    theirs = swap(other, "core")
    (own,) = attend(limits(6), [(unit, own, False)], [from_yx], "attend_far_own")
    attended = combine(limits(0), own, theirs, "combine")

    return gathered_product(
        attended,
        rows_at,
        [w_cols],
        finish_out,
        [jax.ShapeDtypeStruct((rows, HD), BF16)],
        [],
        "output",
    )[0]


def solution(mesh):
    finer = Mesh(mesh.devices.reshape(2, 2, 2, 2, 2, 8), AXES)
    return jax.shard_map(
        per_device,
        mesh=finer,
        in_specs=(P(CTX, HEAD), P(None, HEAD), P(None, HEAD), P(HEAD, None), P()),
        out_specs=P(CTX, HEAD),
        check_vma=False,
    )
```

```python
import itertools
import math

import jax
import jax.numpy as jnp
from jax import lax
from jax.experimental import pallas as pl
from jax.experimental.pallas import tpu as pltpu
from jax.sharding import Mesh
from jax.sharding import PartitionSpec as P

HD = 128
ROWS = 1024
HEAD = ("xl", "z")
CTX = ("yh", "yl", "xh", "core")
AXES = CTX + HEAD
SCORE_BOUND = 24.0
SCALE = SCORE_BOUND * math.log2(math.e)
VMEM = pl.BlockSpec(memory_space=pltpu.VMEM)
SMEM = pl.BlockSpec(memory_space=pltpu.SMEM)
F32 = jnp.float32
BF16 = jnp.bfloat16


def hop(value, axes, target):
    places = list(itertools.product(*(range(lax.axis_size(a)) for a in axes)))
    number = {place: i for i, place in enumerate(places)}
    return lax.ppermute(value, axes, [(number[c], number[tuple(target(*c))]) for c in places])


def swap(value, *axes):
    return hop(value, axes, lambda *c: tuple(1 - i for i in c))


def z_step(value):
    depth = lax.axis_size("z")
    return hop(value, ("core", "z"), lambda c, z: (c, (z + 1 - 2 * c) % depth))


def params(mib):
    return pltpu.CompilerParams(vmem_limit_bytes=mib * 2**20)


def call(kernel, outs, smem_count, args, name, flops, limit=24):
    moved = sum(math.prod(a.shape) * a.dtype.itemsize for a in [*args, *outs])
    return pl.pallas_call(
        kernel,
        out_shape=outs,
        in_specs=[SMEM] * smem_count + [VMEM] * (len(args) - smem_count),
        out_specs=[VMEM] * len(outs),
        compiler_params=params(limit),
        cost_estimate=pl.CostEstimate(flops=flops, bytes_accessed=moved, transcendentals=0),
        name=name,
    )(*args)


def after(value, *others):
    return lax.optimization_barrier((value, *others))[0]


def valid_rows(doc_ref, mask):
    in_doc = (lax.axis_index("yl") * 2 + lax.axis_index("xh")) * 2 + lax.axis_index("core")
    return doc_ref[lax.axis_index("yh")] - (in_doc ^ mask) * ROWS


def contract(weights, jobs, name, finish=None, extras=(), outs=None, smem=()):
    width = sum(w.shape[1] for w in weights)
    flat, plan = [], []
    for total, *terms in jobs:
        plan.append((total is not None, [t[0] for t in terms]))
        flat += ([total] if total is not None else []) + [b for t in terms for b in t[1:]]
    rows = jobs[0][1][1].shape[0]
    tile = 256
    if outs is None:
        outs = [jax.ShapeDtypeStruct((rows, width), F32)] * len(jobs)
    n_s, n_w, n_e, n_f = len(smem), len(weights), len(extras), len(flat)
    depth = lax.axis_size("z")

    def kernel(*refs):
        w_refs = refs[n_s : n_s + n_w]
        e_refs = refs[n_s + n_w : n_s + n_w + n_e]
        b_refs = list(refs[n_s + n_w + n_e : n_s + n_w + n_e + n_f])
        o_refs = refs[n_s + n_w + n_e + n_f :]
        xl, z, core = lax.axis_index("xl"), lax.axis_index("z"), lax.axis_index("core")
        taken = {}

        def weight(step):
            if step not in taken:
                z_at = (z + depth + (2 * core - 1) * step) % depth
                halves = []
                for side in (xl, 1 - xl):
                    first = pl.multiple_of((side * depth + z_at) * HD, HD)
                    halves.append(
                        jnp.concatenate([w[pl.ds(first, HD), :] for w in w_refs], axis=1)
                    )
                taken[step] = jnp.concatenate(halves, axis=0)
            return taken[step]

        for index, (has_total, steps) in enumerate(plan):
            total_ref = b_refs.pop(0) if has_total else None
            pairs = [(s, b_refs.pop(0), b_refs.pop(0)) for s in steps]
            for first in range(0, rows, tile):
                here = slice(first, first + tile)
                total = None if total_ref is None else total_ref[here, :]
                for s, one, two in pairs:
                    both = jnp.concatenate([one[here, :], two[here, :]], axis=1)
                    term = jnp.dot(both, weight(s), preferred_element_type=F32)
                    total = term if total is None else total + term
                if finish is None:
                    o_refs[index][here, :] = total.astype(o_refs[index].dtype)
                else:
                    finish(refs[:n_s], e_refs, o_refs, total, first, tile)

    terms = sum(len(steps) for _, steps in plan)
    return call(
        kernel,
        outs,
        n_s,
        [*smem, *weights, *extras, *flat],
        name,
        2 * rows * 256 * width * terms,
    )


def finish_units(smem, extras, outs, total, first, tile):
    here = slice(first, first + tile)
    total = total + extras[0][here, :]
    proj = total[:, :HD]
    unit = proj * lax.rsqrt(jnp.sum(proj * proj, axis=-1, keepdims=True) + 1e-06)
    row = lax.broadcasted_iota(jnp.int32, (tile, HD), 0) + first
    value = jnp.where(row < valid_rows(smem[0], 0), total[:, HD:], 0.0).astype(BF16)
    unit = unit.astype(BF16)
    outs[0][here, :HD] = unit
    outs[0][here, HD:] = value
    outs[1][here, :] = unit


def finish_out(smem, extras, outs, total, first, tile):
    here = slice(first, first + tile)
    outs[0][here, :] = (total + extras[0][here, :]).astype(BF16)


def attend(doc_lengths, groups, blocks, name, out_type=F32, tile_q=512, tile_k=512):
    masks, blocks = zip(*blocks)
    n_b = len(blocks)
    flat, plan = [], []
    for queries, total, own in groups:
        plan.append((total is not None, own))
        flat += [queries] + ([total] if total is not None else [])
    rows = groups[0][0].shape[0]
    outs = [jax.ShapeDtypeStruct((rows, 2 * HD), out_type)] * len(groups)

    def kernel(*refs):
        limit = [valid_rows(refs[0], mask) for mask in masks]
        kv_refs = refs[1 : 1 + n_b]
        g_refs = list(refs[1 + n_b : 1 + n_b + len(flat)])
        o_refs = refs[1 + n_b + len(flat) :]
        for index, (has_total, own) in enumerate(plan):
            q_ref = g_refs.pop(0)
            t_ref = g_refs.pop(0) if has_total else None

            @pl.loop(0, rows // tile_q)
            def _(step):
                first = pl.multiple_of(step * tile_q, tile_q)
                here = pl.ds(first, tile_q)
                queries = q_ref[here, :]
                total = None if t_ref is None else t_ref[here, :]
                for b, kv in enumerate(kv_refs):
                    for start in range(0, kv.shape[0], tile_k):
                        keys = kv[start : start + tile_k, :HD]
                        values = kv[start : start + tile_k, HD:]
                        row = lax.broadcasted_iota(jnp.int32, (tile_k, HD), 0) + start
                        counted = jnp.where(row < limit[b], 1.0, 0.0).astype(BF16)
                        scores = lax.dot_general(
                            queries, keys, (((1,), (1,)), ((), ())), preferred_element_type=F32
                        )
                        weights = jnp.exp2(scores * SCALE - SCALE)
                        if own and b == 0:
                            q_at = lax.broadcasted_iota(jnp.int32, weights.shape, 0) + first
                            k_at = lax.broadcasted_iota(jnp.int32, weights.shape, 1) + start
                            weights = jnp.where(q_at == k_at, 0.0, weights)
                        term = jnp.dot(
                            weights.astype(BF16),
                            jnp.concatenate([values, counted], axis=1),
                            preferred_element_type=F32,
                        )
                        total = term if total is None else total + term
                o_refs[index][here, :] = total.astype(out_type)

    flops = len(groups) * n_b * 4 * rows * blocks[0].shape[0] * HD * 2
    return call(kernel, outs, 1, [doc_lengths, *blocks, *flat], name, flops)


def combine(doc_lengths, mine, theirs, name):
    rows = mine.shape[0]

    def kernel(doc_ref, a_ref, b_ref, o_ref):
        total = a_ref[...] + b_ref[...].astype(F32)
        row = lax.broadcasted_iota(jnp.int32, (rows, HD), 0)
        valid = row < valid_rows(doc_ref, 0)
        denom = jnp.where(valid, total[:, HD:], 1.0)
        o_ref[...] = jnp.where(valid, total[:, :HD] / denom, 0.0).astype(BF16)

    out = jax.ShapeDtypeStruct((rows, HD), BF16)
    return call(kernel, [out], 1, [doc_lengths, mine, theirs], name, rows * HD * 8)[0]


def column_parts(matrix, count):
    rows, width = matrix.shape[0], matrix.shape[1] // count

    def kernel(m_ref, o_ref):
        for i in range(count):
            o_ref[i] = m_ref[:, i * width : (i + 1) * width]

    out = jax.ShapeDtypeStruct((count, rows, width), matrix.dtype)
    return call(kernel, [out], 0, [matrix], "column_parts", 0)[0]


def gathered_product(block, weights, finish, outs, smem, name):
    half = lax.axis_size("z") // 2
    own, other, cross = [block], [swap(block, "core")], [swap(block, "xl")]
    far = [None]
    total_own = total_other = None
    mine = [(0, own[0], cross[0])]
    for s in range(1, half):
        own_from, other_from, cross_from = own[-1], other[-1], cross[-1]
        if s > 1:
            own_from = after(own_from, cross[s - 2])
            other_from = after(other_from, own[s - 1])
            cross_from = after(cross_from, other[s - 1], *far[s - 2 : s - 1][: s - 2])
        own.append(z_step(own_from))
        other.append(z_step(other_from))
        cross.append(z_step(cross_from))
        far.append(swap(other[s], "xl"))
    own.append(z_step(after(own[-1], cross[half - 2])))
    cross.append(z_step(after(cross[-1], own[half - 1], far[half - 2])))

    for s in range(1, half - 1):
        mine.append((s, own[s], cross[s]))
        mine[0] = (mine[0][0], after(mine[0][1], own[s + 1], other[s + 1], cross[s + 1]), mine[0][2])
        total_own, total_other = contract(
            weights, [[total_own, *mine], [total_other, (s, other[s], far[s])]], f"{name}_{s}"
        )
        mine = []
    last_other = after(other[half - 1], own[half])
    (total_other,) = contract(
        weights, [[total_other, (half - 1, last_other, far[half - 1])]], f"{name}_{half - 1}"
    )
    both = swap(total_other, "core")
    mine += [(s, own[s], cross[s]) for s in (half - 1, half)]
    return contract(
        weights,
        [[total_own, *mine]],
        f"{name}_last",
        finish=finish,
        extras=[both],
        outs=outs,
        smem=smem,
    )


def per_device(tokens, w_query, w_value, w_out, doc_lengths):
    rows = tokens.shape[0]
    heads = lax.axis_size(HEAD)

    joined, unit = gathered_product(
        tokens,
        [w_query, w_value],
        finish_units,
        [jax.ShapeDtypeStruct((rows, 2 * HD), BF16), jax.ShapeDtypeStruct((rows, HD), BF16)],
        [doc_lengths],
        "project",
    )
    unit_other = swap(unit, "core")
    from_y, from_x = swap(joined, "yl"), swap(joined, "xh")
    from_yx = swap(joined, "yl", "xh")
    w_parts = column_parts(w_out, heads)

    own, other = attend(
        doc_lengths, [(unit, None, True), (unit_other, None, False)], [(0, joined)], "attend_own"
    )
    w_cols = lax.all_to_all(after(w_parts, own, from_y, from_x), HEAD, 0, 0)
    w_cols = w_cols.reshape(heads * HD, HD)
    own, other = attend(
        doc_lengths,
        [(unit, own, False), (unit_other, other, False)],
        [(4, from_y), (2, from_x)],
        "attend_near",
    )
    (other,) = attend(
        doc_lengths, [(unit_other, other, False)], [(6, from_yx)], "attend_far_other", out_type=BF16
    )
    theirs = swap(other, "core")
    (own,) = attend(doc_lengths, [(unit, own, False)], [(6, from_yx)], "attend_far_own")
    attended = combine(doc_lengths, after(own, w_cols), theirs, "combine")

    return gathered_product(
        attended,
        [w_cols],
        finish_out,
        [jax.ShapeDtypeStruct((rows, HD), BF16)],
        [],
        "output",
    )[0]


def solution(mesh):
    finer = Mesh(mesh.devices.reshape(2, 2, 2, 2, 2, 8), AXES)
    return jax.shard_map(
        per_device,
        mesh=finer,
        in_specs=(P(CTX, HEAD), P(None, HEAD), P(None, HEAD), P(HEAD, None), P()),
        out_specs=P(CTX, HEAD),
        check_vma=False,
    )
```

```python
import itertools
import math

import jax
import jax.numpy as jnp
from jax import lax
from jax.experimental import pallas as pl
from jax.experimental.pallas import tpu as pltpu
from jax.sharding import Mesh
from jax.sharding import PartitionSpec as P

HD = 128
ROWS = 1024
HEAD = ("xl", "z")
CTX = ("yh", "yl", "xh", "core")
AXES = CTX + HEAD
SCORE_BOUND = 24.0
SCALE = SCORE_BOUND * math.log2(math.e)
VMEM = pl.BlockSpec(memory_space=pltpu.VMEM)
SMEM = pl.BlockSpec(memory_space=pltpu.SMEM)
F32 = jnp.float32
BF16 = jnp.bfloat16


def hop(value, axes, target):
    places = list(itertools.product(*(range(lax.axis_size(a)) for a in axes)))
    number = {place: i for i, place in enumerate(places)}
    return lax.ppermute(value, axes, [(number[c], number[tuple(target(*c))]) for c in places])


def swap(value, *axes):
    return hop(value, axes, lambda *c: tuple(1 - i for i in c))


def z_step(value):
    depth = lax.axis_size("z")
    return hop(value, ("core", "z"), lambda c, z: (c, (z + 1 - 2 * c) % depth))


def params(mib):
    return pltpu.CompilerParams(vmem_limit_bytes=mib * 2**20)


def call(kernel, outs, smem_count, args, name, flops, limit=24):
    moved = sum(math.prod(a.shape) * a.dtype.itemsize for a in [*args, *outs])
    return pl.pallas_call(
        kernel,
        out_shape=outs,
        in_specs=[SMEM] * smem_count + [VMEM] * (len(args) - smem_count),
        out_specs=[VMEM] * len(outs),
        compiler_params=params(limit),
        cost_estimate=pl.CostEstimate(flops=flops, bytes_accessed=moved, transcendentals=0),
        name=name,
    )(*args)


def after(value, *others):
    return lax.optimization_barrier((value, *others))[0]


def valid_rows(doc_ref, mask):
    in_doc = (lax.axis_index("yl") * 2 + lax.axis_index("xh")) * 2 + lax.axis_index("core")
    return doc_ref[lax.axis_index("yh")] - (in_doc ^ mask) * ROWS


def contract(weights, jobs, name, place=lambda head: head, finish=None, extras=(), outs=None, smem=()):
    width = sum(w.shape[1] for w in weights)
    flat, plan = [], []
    for total, *terms in jobs:
        plan.append((total is not None, [t[0] for t in terms]))
        flat += ([total] if total is not None else []) + [b for t in terms for b in t[1:]]
    rows = jobs[0][1][1].shape[0]
    tile = 256
    if outs is None:
        outs = [jax.ShapeDtypeStruct((rows, width), F32)] * len(jobs)
    n_s, n_w, n_e, n_f = len(smem), len(weights), len(extras), len(flat)
    depth = lax.axis_size("z")

    def kernel(*refs):
        w_refs = refs[n_s : n_s + n_w]
        e_refs = refs[n_s + n_w : n_s + n_w + n_e]
        b_refs = list(refs[n_s + n_w + n_e : n_s + n_w + n_e + n_f])
        o_refs = refs[n_s + n_w + n_e + n_f :]
        xl, z, core = lax.axis_index("xl"), lax.axis_index("z"), lax.axis_index("core")
        taken = {}

        def weight(step):
            if step not in taken:
                z_at = (z + depth + (2 * core - 1) * step) % depth
                halves = []
                for side in (xl, 1 - xl):
                    first = pl.multiple_of(place(side * depth + z_at) * HD, HD)
                    halves.append(
                        jnp.concatenate([w[pl.ds(first, HD), :] for w in w_refs], axis=1)
                    )
                taken[step] = jnp.concatenate(halves, axis=0)
            return taken[step]

        for index, (has_total, steps) in enumerate(plan):
            total_ref = b_refs.pop(0) if has_total else None
            pairs = [(s, b_refs.pop(0), b_refs.pop(0)) for s in steps]
            for first in range(0, rows, tile):
                here = slice(first, first + tile)
                total = None if total_ref is None else total_ref[here, :]
                for s, one, two in pairs:
                    both = jnp.concatenate([one[here, :], two[here, :]], axis=1)
                    term = jnp.dot(both, weight(s), preferred_element_type=F32)
                    total = term if total is None else total + term
                if finish is None:
                    o_refs[index][here, :] = total.astype(o_refs[index].dtype)
                else:
                    finish(refs[:n_s], e_refs, o_refs, total, first, tile)

    terms = sum(len(steps) for _, steps in plan)
    return call(
        kernel,
        outs,
        n_s,
        [*smem, *weights, *extras, *flat],
        name,
        2 * rows * 256 * width * terms,
    )


def finish_units(smem, extras, outs, total, first, tile):
    here = slice(first, first + tile)
    total = total + extras[0][here, :]
    proj = total[:, :HD]
    unit = proj * lax.rsqrt(jnp.sum(proj * proj, axis=-1, keepdims=True) + 1e-06)
    row = lax.broadcasted_iota(jnp.int32, (tile, HD), 0) + first
    value = jnp.where(row < valid_rows(smem[0], 0), total[:, HD:], 0.0).astype(BF16)
    unit = unit.astype(BF16)
    outs[0][here, :HD] = unit
    outs[0][here, HD:] = value
    outs[1][here, :] = unit


def finish_out(smem, extras, outs, total, first, tile):
    here = slice(first, first + tile)
    outs[0][here, :] = (total + extras[0][here, :]).astype(BF16)


def attend(doc_lengths, groups, blocks, name, out_type=F32, tile_q=512, tile_k=512):
    masks, blocks = zip(*blocks)
    n_b = len(blocks)
    flat, plan = [], []
    for queries, total, own in groups:
        plan.append((total is not None, own))
        flat += [queries] + ([total] if total is not None else [])
    rows = groups[0][0].shape[0]
    outs = [jax.ShapeDtypeStruct((rows, 2 * HD), out_type)] * len(groups)

    def kernel(*refs):
        limit = [valid_rows(refs[0], mask) for mask in masks]
        kv_refs = refs[1 : 1 + n_b]
        g_refs = list(refs[1 + n_b : 1 + n_b + len(flat)])
        o_refs = refs[1 + n_b + len(flat) :]
        for index, (has_total, own) in enumerate(plan):
            q_ref = g_refs.pop(0)
            t_ref = g_refs.pop(0) if has_total else None

            @pl.loop(0, rows // tile_q)
            def _(step):
                first = pl.multiple_of(step * tile_q, tile_q)
                here = pl.ds(first, tile_q)
                queries = q_ref[here, :]
                total = None if t_ref is None else t_ref[here, :]
                for b, kv in enumerate(kv_refs):
                    for start in range(0, kv.shape[0], tile_k):
                        keys = kv[start : start + tile_k, :HD]
                        values = kv[start : start + tile_k, HD:]
                        row = lax.broadcasted_iota(jnp.int32, (tile_k, HD), 0) + start
                        counted = jnp.where(row < limit[b], 1.0, 0.0).astype(BF16)
                        scores = lax.dot_general(
                            queries, keys, (((1,), (1,)), ((), ())), preferred_element_type=F32
                        )
                        weights = jnp.exp2(scores * SCALE - SCALE)
                        if own and b == 0:
                            q_at = lax.broadcasted_iota(jnp.int32, weights.shape, 0) + first
                            k_at = lax.broadcasted_iota(jnp.int32, weights.shape, 1) + start
                            weights = jnp.where(q_at == k_at, 0.0, weights)
                        term = jnp.dot(
                            weights.astype(BF16),
                            jnp.concatenate([values, counted], axis=1),
                            preferred_element_type=F32,
                        )
                        total = term if total is None else total + term
                o_refs[index][here, :] = total.astype(out_type)

    flops = len(groups) * n_b * 4 * rows * blocks[0].shape[0] * HD * 2
    return call(kernel, outs, 1, [doc_lengths, *blocks, *flat], name, flops)


def combine(doc_lengths, mine, theirs, name):
    rows = mine.shape[0]

    def kernel(doc_ref, a_ref, b_ref, o_ref):
        total = a_ref[...] + b_ref[...].astype(F32)
        row = lax.broadcasted_iota(jnp.int32, (rows, HD), 0)
        valid = row < valid_rows(doc_ref, 0)
        denom = jnp.where(valid, total[:, HD:], 1.0)
        o_ref[...] = jnp.where(valid, total[:, :HD] / denom, 0.0).astype(BF16)

    out = jax.ShapeDtypeStruct((rows, HD), BF16)
    return call(kernel, [out], 1, [doc_lengths, mine, theirs], name, rows * HD * 8)[0]


def own_columns(w_out):
    heads = lax.axis_size(HEAD)
    depth = lax.axis_size("z")

    def picked(w):
        def kernel(w_ref, o_ref):
            head = lax.axis_index("xl") * depth + lax.axis_index("z")
            to = (head + heads - ctx_index()) % heads
            o_ref[...] = w_ref[:, pl.ds(pl.multiple_of(to * HD, HD), HD)]

        out = jax.ShapeDtypeStruct((w.shape[0], HD), w.dtype)
        return call(kernel, [out], 0, [w], "pick_columns", 0)[0]

    def turned(yh, yl, xh, core, xl, z):
        to = (xl * depth + z - (((yh * 2 + yl) * 2 + xh) * 2 + core)) % heads
        return yh, yl, xh, core, to // depth, to % depth

    def joined(one, two):
        rows = one.shape[0]

        def kernel(a_ref, b_ref, o_ref):
            o_ref[:rows] = a_ref[...]
            o_ref[rows:] = b_ref[...]

        out = jax.ShapeDtypeStruct((2 * rows, HD), one.dtype)
        return call(kernel, [out], 0, [one, two], "join_columns", 0)[0]

    stages = [lambda gate: hop(picked(after(w_out, gate)), AXES, turned)]
    held = []

    def exchange(axis):
        def stage(gate):
            value = held[-1]
            return joined(value, swap(after(value, gate), axis))

        return stage

    stages += [exchange(axis) for axis in ("yh", "yl", "xh", "core")]

    def advance(gate):
        held.append(stages[len(held)](gate))
        return held[-1]

    return advance


def ctx_index():
    in_doc = (lax.axis_index("yl") * 2 + lax.axis_index("xh")) * 2 + lax.axis_index("core")
    return lax.axis_index("yh") * 8 + in_doc


def column_place(head):
    heads = lax.axis_size(HEAD)
    own = lax.axis_index("xl") * lax.axis_size("z") + lax.axis_index("z")
    away = ((head + heads - own) % heads) ^ ctx_index()
    return (away & 1) * 8 + (away & 2) * 2 + (away & 4) // 2 + (away & 8) // 8


def gathered_product(block, weights, finish, outs, smem, name, place=lambda head: head, beside=None):
    half = lax.axis_size("z") // 2
    own, other, cross = [block], [swap(block, "core")], [swap(block, "xl")]
    far, side = [None], []
    if beside is not None:
        side.append(beside(other[0]))
    total_own = total_other = None
    mine = [(0, own[0], cross[0])]
    for s in range(1, half):
        own_from, other_from, cross_from = own[-1], other[-1], cross[-1]
        if s == 2:
            other_from = after(other_from, own[1])
            own_from = after(own_from, other[1], cross[1], *side[0:1])
        if s == 3:
            other_from = after(other_from, own[2])
            own_from = after(own_from, other[2], cross[1], far[1], *side[2:3])
        other.append(z_step(other_from))
        far.append(swap(other[s], "xl"))
        own.append(z_step(own_from))
        if s == 2:
            cross_from = after(cross_from, other[2])
        if s == 3:
            cross_from = after(cross_from, other[3], far[2])
        cross.append(z_step(cross_from))
        if beside is not None and s == 1:
            side.append(beside(own[1]))
            side.append(beside(own[1]))
        if beside is not None and s == 2:
            side.append(beside(other[2]))
    own.append(z_step(after(own[-1], cross[half - 2], other[half - 1], *side[3:4])))
    cross.append(z_step(after(cross[-1], own[half - 1], far[half - 1])))

    for s in range(1, half - 1):
        mine.append((s, own[s], cross[s]))
        mine[0] = (mine[0][0], after(mine[0][1], own[s + 1], other[s + 1], cross[s + 1]), mine[0][2])
        total_own, total_other = contract(
            weights,
            [[total_own, *mine], [total_other, (s, other[s], far[s])]],
            f"{name}_{s}",
            place,
        )
        mine = []
    last_other = after(other[half - 1], own[half])
    (total_other,) = contract(
        weights,
        [[total_other, (half - 1, last_other, far[half - 1])]],
        f"{name}_{half - 1}",
        place,
    )
    both = swap(total_other, "core")
    mine += [(s, own[s], cross[s]) for s in (half - 1, half)]
    results = contract(
        weights,
        [[total_own, *mine]],
        f"{name}_last",
        place,
        finish=finish,
        extras=[both],
        outs=outs,
        smem=smem,
    )
    return results


def per_device(tokens, w_query, w_value, w_out, doc_lengths):
    rows = tokens.shape[0]
    columns = own_columns(w_out)
    joined, unit = gathered_product(
        tokens,
        [w_query, w_value],
        finish_units,
        [jax.ShapeDtypeStruct((rows, 2 * HD), BF16), jax.ShapeDtypeStruct((rows, HD), BF16)],
        [doc_lengths],
        "project",
        beside=columns,
    )
    unit_other = swap(unit, "core")
    from_y, from_x = swap(joined, "yl"), swap(joined, "xh")
    from_yx = swap(joined, "yl", "xh")
    w_cols = columns(from_y)

    own, other = attend(
        doc_lengths, [(unit, None, True), (unit_other, None, False)], [(0, joined)], "attend_own"
    )
    own, other = attend(
        doc_lengths,
        [(unit, own, False), (unit_other, other, False)],
        [(4, from_y), (2, from_x)],
        "attend_near",
    )
    (other,) = attend(
        doc_lengths, [(unit_other, other, False)], [(6, from_yx)], "attend_far_other", out_type=BF16
    )
    theirs = swap(other, "core")
    (own,) = attend(doc_lengths, [(unit, own, False)], [(6, from_yx)], "attend_far_own")
    attended = combine(doc_lengths, after(own, w_cols), theirs, "combine")

    return gathered_product(
        attended,
        [w_cols],
        finish_out,
        [jax.ShapeDtypeStruct((rows, HD), BF16)],
        [],
        "output",
        column_place,
    )[0]


def solution(mesh):
    finer = Mesh(mesh.devices.reshape(2, 2, 2, 2, 2, 8), AXES)
    return jax.shard_map(
        per_device,
        mesh=finer,
        in_specs=(P(CTX, HEAD), P(None, HEAD), P(None, HEAD), P(HEAD, None), P()),
        out_specs=P(CTX, HEAD),
        check_vma=False,
    )
```

```python
import itertools
import math

import jax
import jax.numpy as jnp
from jax import lax
from jax.experimental import pallas as pl
from jax.experimental.pallas import tpu as pltpu
from jax.sharding import Mesh
from jax.sharding import PartitionSpec as P

HD = 128
ROWS = 1024
HEAD = ("xl", "z")
CTX = ("yh", "yl", "xh", "core")
AXES = CTX + HEAD
SCORE_BOUND = 24.0
SCALE = SCORE_BOUND * math.log2(math.e)
VMEM = pl.BlockSpec(memory_space=pltpu.VMEM)
SMEM = pl.BlockSpec(memory_space=pltpu.SMEM)
F32 = jnp.float32
BF16 = jnp.bfloat16


def hop(value, axes, target):
    places = list(itertools.product(*(range(lax.axis_size(a)) for a in axes)))
    number = {place: i for i, place in enumerate(places)}
    return lax.ppermute(value, axes, [(number[c], number[tuple(target(*c))]) for c in places])


def swap(value, *axes):
    return hop(value, axes, lambda *c: tuple(1 - i for i in c))


def z_step(value):
    depth = lax.axis_size("z")
    return hop(value, ("core", "z"), lambda c, z: (c, (z + 1 - 2 * c) % depth))


def params(mib):
    return pltpu.CompilerParams(vmem_limit_bytes=mib * 2**20)


def call(kernel, outs, smem_count, args, name, flops, limit=24):
    moved = sum(math.prod(a.shape) * a.dtype.itemsize for a in [*args, *outs])
    return pl.pallas_call(
        kernel,
        out_shape=outs,
        in_specs=[SMEM] * smem_count + [VMEM] * (len(args) - smem_count),
        out_specs=[VMEM] * len(outs),
        compiler_params=params(limit),
        cost_estimate=pl.CostEstimate(flops=flops, bytes_accessed=moved, transcendentals=0),
        name=name,
    )(*args)


def after(value, *others):
    return lax.optimization_barrier((value, *others))[0]


def valid_rows(doc_ref, mask):
    in_doc = (lax.axis_index("yl") * 2 + lax.axis_index("xh")) * 2 + lax.axis_index("core")
    return doc_ref[lax.axis_index("yh")] - (in_doc ^ mask) * ROWS


def contract(weights, jobs, name, finish=None, extras=(), outs=None, smem=()):
    width = sum(w.shape[1] for w in weights)
    flat, plan = [], []
    for total, *terms in jobs:
        plan.append((total is not None, [t[0] for t in terms]))
        flat += ([total] if total is not None else []) + [b for t in terms for b in t[1:]]
    rows = jobs[0][1][1].shape[0]
    tile = 256
    if outs is None:
        outs = [jax.ShapeDtypeStruct((rows, width), F32)] * len(jobs)
    n_s, n_w, n_e, n_f = len(smem), len(weights), len(extras), len(flat)
    depth = lax.axis_size("z")

    def kernel(*refs):
        w_refs = refs[n_s : n_s + n_w]
        e_refs = refs[n_s + n_w : n_s + n_w + n_e]
        b_refs = list(refs[n_s + n_w + n_e : n_s + n_w + n_e + n_f])
        o_refs = refs[n_s + n_w + n_e + n_f :]
        xl, z, core = lax.axis_index("xl"), lax.axis_index("z"), lax.axis_index("core")
        taken = {}

        def weight(step):
            if step not in taken:
                z_at = (z + depth + (2 * core - 1) * step) % depth
                halves = []
                for side in (xl, 1 - xl):
                    first = pl.multiple_of((side * depth + z_at) * HD, HD)
                    halves.append(
                        jnp.concatenate([w[pl.ds(first, HD), :] for w in w_refs], axis=1)
                    )
                taken[step] = jnp.concatenate(halves, axis=0)
            return taken[step]

        for index, (has_total, steps) in enumerate(plan):
            total_ref = b_refs.pop(0) if has_total else None
            pairs = [(s, b_refs.pop(0), b_refs.pop(0)) for s in steps]
            for first in range(0, rows, tile):
                here = slice(first, first + tile)
                total = None if total_ref is None else total_ref[here, :]
                for s, one, two in pairs:
                    both = jnp.concatenate([one[here, :], two[here, :]], axis=1)
                    term = jnp.dot(both, weight(s), preferred_element_type=F32)
                    total = term if total is None else total + term
                if finish is None:
                    o_refs[index][here, :] = total.astype(o_refs[index].dtype)
                else:
                    finish(refs[:n_s], e_refs, o_refs, total, first, tile)

    terms = sum(len(steps) for _, steps in plan)
    return call(
        kernel,
        outs,
        n_s,
        [*smem, *weights, *extras, *flat],
        name,
        2 * rows * 256 * width * terms,
    )


def finish_units(smem, extras, outs, total, first, tile):
    here = slice(first, first + tile)
    total = total + extras[0][here, :]
    proj = total[:, :HD]
    unit = proj * lax.rsqrt(jnp.sum(proj * proj, axis=-1, keepdims=True) + 1e-06)
    row = lax.broadcasted_iota(jnp.int32, (tile, HD), 0) + first
    value = jnp.where(row < valid_rows(smem[0], 0), total[:, HD:], 0.0).astype(BF16)
    unit = unit.astype(BF16)
    outs[0][here, :HD] = unit
    outs[0][here, HD:] = value
    outs[1][here, :] = unit


def finish_out(smem, extras, outs, total, first, tile):
    here = slice(first, first + tile)
    outs[0][here, :] = (total + extras[0][here, :]).astype(BF16)


def attend(doc_lengths, groups, blocks, name, out_type=F32, tile_q=512, tile_k=512):
    masks, blocks = zip(*blocks)
    n_b = len(blocks)
    flat, plan = [], []
    for queries, total, own in groups:
        plan.append((total is not None, own))
        flat += [queries] + ([total] if total is not None else [])
    rows = groups[0][0].shape[0]
    outs = [jax.ShapeDtypeStruct((rows, 2 * HD), out_type)] * len(groups)

    def kernel(*refs):
        limit = [valid_rows(refs[0], mask) for mask in masks]
        kv_refs = refs[1 : 1 + n_b]
        g_refs = list(refs[1 + n_b : 1 + n_b + len(flat)])
        o_refs = refs[1 + n_b + len(flat) :]
        for index, (has_total, own) in enumerate(plan):
            q_ref = g_refs.pop(0)
            t_ref = g_refs.pop(0) if has_total else None

            @pl.loop(0, rows // tile_q)
            def _(step):
                first = pl.multiple_of(step * tile_q, tile_q)
                here = pl.ds(first, tile_q)
                queries = q_ref[here, :]
                total = None if t_ref is None else t_ref[here, :]
                for b, kv in enumerate(kv_refs):
                    for start in range(0, kv.shape[0], tile_k):
                        keys = kv[start : start + tile_k, :HD]
                        values = kv[start : start + tile_k, HD:]
                        row = lax.broadcasted_iota(jnp.int32, (tile_k, HD), 0) + start
                        counted = jnp.where(row < limit[b], 1.0, 0.0).astype(BF16)
                        scores = lax.dot_general(
                            queries, keys, (((1,), (1,)), ((), ())), preferred_element_type=F32
                        )
                        weights = jnp.exp2(scores * SCALE - SCALE)
                        if own and b == 0:
                            q_at = lax.broadcasted_iota(jnp.int32, weights.shape, 0) + first
                            k_at = lax.broadcasted_iota(jnp.int32, weights.shape, 1) + start
                            weights = jnp.where(q_at == k_at, 0.0, weights)
                        term = jnp.dot(
                            weights.astype(BF16),
                            jnp.concatenate([values, counted], axis=1),
                            preferred_element_type=F32,
                        )
                        total = term if total is None else total + term
                o_refs[index][here, :] = total.astype(out_type)

    flops = len(groups) * n_b * 4 * rows * blocks[0].shape[0] * HD * 2
    return call(kernel, outs, 1, [doc_lengths, *blocks, *flat], name, flops)


def combine(doc_lengths, mine, theirs, name):
    rows = mine.shape[0]

    def kernel(doc_ref, a_ref, b_ref, o_ref):
        total = a_ref[...] + b_ref[...].astype(F32)
        row = lax.broadcasted_iota(jnp.int32, (rows, HD), 0)
        valid = row < valid_rows(doc_ref, 0)
        denom = jnp.where(valid, total[:, HD:], 1.0)
        o_ref[...] = jnp.where(valid, total[:, :HD] / denom, 0.0).astype(BF16)

    out = jax.ShapeDtypeStruct((rows, HD), BF16)
    return call(kernel, [out], 1, [doc_lengths, mine, theirs], name, rows * HD * 8)[0]


def column_parts(matrix, count):
    rows, width = matrix.shape[0], matrix.shape[1] // count

    def kernel(m_ref, o_ref):
        for i in range(count):
            o_ref[i] = m_ref[:, i * width : (i + 1) * width]

    out = jax.ShapeDtypeStruct((count, rows, width), matrix.dtype)
    return call(kernel, [out], 0, [matrix], "column_parts", 0)[0]


def gathered_product(block, weights, finish, outs, smem, name):
    half = lax.axis_size("z") // 2
    own, other, cross = [block], [swap(block, "core")], [swap(block, "xl")]
    far = [None]
    total_own = total_other = None
    mine = [(0, own[0], cross[0])]
    for s in range(1, half):
        own_from, other_from, cross_from = own[-1], other[-1], cross[-1]
        if s > 1:
            own_from = after(own_from, cross[s - 2])
            other_from = after(other_from, own[s - 1])
            cross_from = after(cross_from, other[s - 1])
        own.append(z_step(own_from))
        other.append(z_step(other_from))
        cross.append(z_step(cross_from))
        far.append(swap(other[s], "xl"))
    own.append(z_step(after(own[-1], cross[half - 2], far[1])))
    cross.append(z_step(after(cross[-1], own[half - 1], far[2])))

    total_own, total_other = contract(
        weights,
        [
            [None, *mine, (1, own[1], after(cross[1], own[3], other[3], cross[3]))],
            [None, (1, other[1], far[1])],
        ],
        f"{name}_1",
    )
    last_other = after(other[3], own[4], cross[4], total_own)
    total_own, total_other = contract(
        weights,
        [
            [total_own, (2, own[2], cross[2])],
            [total_other, (2, other[2], far[2]), (3, last_other, far[3])],
        ],
        f"{name}_2",
    )
    mine = []
    both = swap(total_other, "core")
    mine += [(s, own[s], cross[s]) for s in (half - 1, half)]
    return contract(
        weights,
        [[total_own, *mine]],
        f"{name}_last",
        finish=finish,
        extras=[both],
        outs=outs,
        smem=smem,
    )


def per_device(tokens, w_query, w_value, w_out, doc_lengths):
    rows = tokens.shape[0]
    heads = lax.axis_size(HEAD)

    joined, unit = gathered_product(
        tokens,
        [w_query, w_value],
        finish_units,
        [jax.ShapeDtypeStruct((rows, 2 * HD), BF16), jax.ShapeDtypeStruct((rows, HD), BF16)],
        [doc_lengths],
        "project",
    )
    unit_other = swap(unit, "core")
    from_y, from_x = swap(joined, "yl"), swap(joined, "xh")
    from_yx = swap(joined, "yl", "xh")
    w_parts = column_parts(w_out, heads)

    own, other = attend(
        doc_lengths, [(unit, None, True), (unit_other, None, False)], [(0, joined)], "attend_own"
    )
    w_cols = lax.all_to_all(after(w_parts, own, from_y, from_x), HEAD, 0, 0)
    w_cols = w_cols.reshape(heads * HD, HD)
    own, other = attend(
        doc_lengths,
        [(unit, own, False), (unit_other, other, False)],
        [(4, from_y), (2, from_x)],
        "attend_near",
    )
    (other,) = attend(
        doc_lengths, [(unit_other, other, False)], [(6, from_yx)], "attend_far_other", out_type=BF16
    )
    theirs = swap(other, "core")
    (own,) = attend(doc_lengths, [(unit, own, False)], [(6, from_yx)], "attend_far_own")
    attended = combine(doc_lengths, after(own, w_cols), theirs, "combine")

    return gathered_product(
        attended,
        [w_cols],
        finish_out,
        [jax.ShapeDtypeStruct((rows, HD), BF16)],
        [],
        "output",
    )[0]


def solution(mesh):
    finer = Mesh(mesh.devices.reshape(2, 2, 2, 2, 2, 8), AXES)
    return jax.shard_map(
        per_device,
        mesh=finer,
        in_specs=(P(CTX, HEAD), P(None, HEAD), P(None, HEAD), P(HEAD, None), P()),
        out_specs=P(CTX, HEAD),
        check_vma=False,
    )
```

```python
import itertools
import math

import jax
import jax.numpy as jnp
from jax import lax
from jax.experimental import pallas as pl
from jax.experimental.pallas import tpu as pltpu
from jax.sharding import Mesh
from jax.sharding import PartitionSpec as P

HD = 128
ROWS = 1024
HEAD = ("xl", "z")
CTX = ("yh", "yl", "xh", "core")
AXES = CTX + HEAD
SCORE_BOUND = 24.0
SCALE = SCORE_BOUND * math.log2(math.e)
VMEM = pl.BlockSpec(memory_space=pltpu.VMEM)
SMEM = pl.BlockSpec(memory_space=pltpu.SMEM)
F32 = jnp.float32
BF16 = jnp.bfloat16


def hop(value, axes, target):
    places = list(itertools.product(*(range(lax.axis_size(a)) for a in axes)))
    number = {place: i for i, place in enumerate(places)}
    return lax.ppermute(value, axes, [(number[c], number[tuple(target(*c))]) for c in places])


def swap(value, *axes):
    return hop(value, axes, lambda *c: tuple(1 - i for i in c))


def z_step(value):
    depth = lax.axis_size("z")
    return hop(value, ("core", "z"), lambda c, z: (c, (z + 1 - 2 * c) % depth))


def params(mib):
    return pltpu.CompilerParams(vmem_limit_bytes=mib * 2**20)


def call(kernel, outs, smem_count, args, name, flops, limit=24):
    moved = sum(math.prod(a.shape) * a.dtype.itemsize for a in [*args, *outs])
    return pl.pallas_call(
        kernel,
        out_shape=outs,
        in_specs=[SMEM] * smem_count + [VMEM] * (len(args) - smem_count),
        out_specs=[VMEM] * len(outs),
        compiler_params=params(limit),
        cost_estimate=pl.CostEstimate(flops=flops, bytes_accessed=moved, transcendentals=0),
        name=name,
    )(*args)


def after(value, *others):
    return lax.optimization_barrier((value, *others))[0]


def valid_rows(doc_ref, mask):
    in_doc = (lax.axis_index("yl") * 2 + lax.axis_index("xh")) * 2 + lax.axis_index("core")
    return doc_ref[lax.axis_index("yh")] - (in_doc ^ mask) * ROWS


def contract(weights, jobs, name, finish=None, extras=(), outs=None, smem=()):
    width = sum(w.shape[1] for w in weights)
    flat, plan = [], []
    for total, *terms in jobs:
        plan.append((total is not None, [t[0] for t in terms]))
        flat += ([total] if total is not None else []) + [b for t in terms for b in t[1:]]
    rows = jobs[0][1][1].shape[0]
    tile = 256
    if outs is None:
        outs = [jax.ShapeDtypeStruct((rows, width), F32)] * len(jobs)
    n_s, n_w, n_e, n_f = len(smem), len(weights), len(extras), len(flat)
    depth = lax.axis_size("z")

    def kernel(*refs):
        w_refs = refs[n_s : n_s + n_w]
        e_refs = refs[n_s + n_w : n_s + n_w + n_e]
        b_refs = list(refs[n_s + n_w + n_e : n_s + n_w + n_e + n_f])
        o_refs = refs[n_s + n_w + n_e + n_f :]
        xl, z, core = lax.axis_index("xl"), lax.axis_index("z"), lax.axis_index("core")
        taken = {}

        def weight(step):
            if step not in taken:
                z_at = (z + depth + (2 * core - 1) * step) % depth
                halves = []
                for side in (xl, 1 - xl):
                    first = pl.multiple_of((side * depth + z_at) * HD, HD)
                    halves.append(
                        jnp.concatenate([w[pl.ds(first, HD), :] for w in w_refs], axis=1)
                    )
                taken[step] = jnp.concatenate(halves, axis=0)
            return taken[step]

        for index, (has_total, steps) in enumerate(plan):
            total_ref = b_refs.pop(0) if has_total else None
            pairs = [(s, b_refs.pop(0), b_refs.pop(0)) for s in steps]
            for first in range(0, rows, tile):
                here = slice(first, first + tile)
                total = None if total_ref is None else total_ref[here, :]
                for s, one, two in pairs:
                    both = jnp.concatenate([one[here, :], two[here, :]], axis=1)
                    term = jnp.dot(both, weight(s), preferred_element_type=F32)
                    total = term if total is None else total + term
                if finish is None:
                    o_refs[index][here, :] = total.astype(o_refs[index].dtype)
                else:
                    finish(refs[:n_s], e_refs, o_refs, total, first, tile)

    terms = sum(len(steps) for _, steps in plan)
    return call(
        kernel,
        outs,
        n_s,
        [*smem, *weights, *extras, *flat],
        name,
        2 * rows * 256 * width * terms,
    )


def finish_units(smem, extras, outs, total, first, tile):
    here = slice(first, first + tile)
    total = total + extras[0][here, :]
    proj = total[:, :HD]
    unit = proj * lax.rsqrt(jnp.sum(proj * proj, axis=-1, keepdims=True) + 1e-06)
    row = lax.broadcasted_iota(jnp.int32, (tile, HD), 0) + first
    value = jnp.where(row < valid_rows(smem[0], 0), total[:, HD:], 0.0).astype(BF16)
    unit = unit.astype(BF16)
    outs[0][here, :HD] = unit
    outs[0][here, HD:] = value
    outs[1][here, :] = unit


def finish_out(smem, extras, outs, total, first, tile):
    here = slice(first, first + tile)
    outs[0][here, :] = (total + extras[0][here, :]).astype(BF16)


def attend(doc_lengths, groups, blocks, name, out_type=F32, tile_q=512, tile_k=512):
    masks, blocks = zip(*blocks)
    n_b = len(blocks)
    flat, plan = [], []
    for queries, total, own in groups:
        plan.append((total is not None, own))
        flat += [queries] + ([total] if total is not None else [])
    rows = groups[0][0].shape[0]
    outs = [jax.ShapeDtypeStruct((rows, 2 * HD), out_type)] * len(groups)

    def kernel(*refs):
        limit = [valid_rows(refs[0], mask) for mask in masks]
        kv_refs = refs[1 : 1 + n_b]
        g_refs = list(refs[1 + n_b : 1 + n_b + len(flat)])
        o_refs = refs[1 + n_b + len(flat) :]
        for index, (has_total, own) in enumerate(plan):
            q_ref = g_refs.pop(0)
            t_ref = g_refs.pop(0) if has_total else None

            @pl.loop(0, rows // tile_q)
            def _(step):
                first = pl.multiple_of(step * tile_q, tile_q)
                here = pl.ds(first, tile_q)
                queries = q_ref[here, :]
                total = None if t_ref is None else t_ref[here, :]
                for b, kv in enumerate(kv_refs):
                    for start in range(0, kv.shape[0], tile_k):
                        keys = kv[start : start + tile_k, :HD]
                        values = kv[start : start + tile_k, HD:]
                        row = lax.broadcasted_iota(jnp.int32, (tile_k, HD), 0) + start
                        counted = jnp.where(row < limit[b], 1.0, 0.0).astype(BF16)
                        scores = lax.dot_general(
                            queries, keys, (((1,), (1,)), ((), ())), preferred_element_type=F32
                        )
                        weights = jnp.exp2(scores * SCALE - SCALE)
                        if own and b == 0:
                            q_at = lax.broadcasted_iota(jnp.int32, weights.shape, 0) + first
                            k_at = lax.broadcasted_iota(jnp.int32, weights.shape, 1) + start
                            weights = jnp.where(q_at == k_at, 0.0, weights)
                        term = jnp.dot(
                            weights.astype(BF16),
                            jnp.concatenate([values, counted], axis=1),
                            preferred_element_type=F32,
                        )
                        total = term if total is None else total + term
                o_refs[index][here, :] = total.astype(out_type)

    flops = len(groups) * n_b * 4 * rows * blocks[0].shape[0] * HD * 2
    return call(kernel, outs, 1, [doc_lengths, *blocks, *flat], name, flops)


def combine(doc_lengths, mine, theirs, name):
    rows = mine.shape[0]

    def kernel(doc_ref, a_ref, b_ref, o_ref):
        total = a_ref[...] + b_ref[...].astype(F32)
        row = lax.broadcasted_iota(jnp.int32, (rows, HD), 0)
        valid = row < valid_rows(doc_ref, 0)
        denom = jnp.where(valid, total[:, HD:], 1.0)
        o_ref[...] = jnp.where(valid, total[:, :HD] / denom, 0.0).astype(BF16)

    out = jax.ShapeDtypeStruct((rows, HD), BF16)
    return call(kernel, [out], 1, [doc_lengths, mine, theirs], name, rows * HD * 8)[0]


def column_parts(matrix, count):
    rows, width = matrix.shape[0], matrix.shape[1] // count

    def kernel(m_ref, o_ref):
        for i in range(count):
            o_ref[i] = m_ref[:, i * width : (i + 1) * width]

    out = jax.ShapeDtypeStruct((count, rows, width), matrix.dtype)
    return call(kernel, [out], 0, [matrix], "column_parts", 0)[0]


def gathered_product(block, weights, finish, outs, smem, name):
    assert lax.axis_size("z") == 8
    own, other = [block], [swap(block, "core")]
    cross, far = [swap(after(block, other[0]), "xl")], [None]
    mine = [(0, own[0], cross[0])]
    own.append(z_step(own[0]))
    other.append(z_step(other[0]))
    far.append(swap(other[1], "xl"))
    own.append(z_step(own[1]))
    cross.append(z_step(after(cross[0], other[1])))
    other.append(z_step(after(other[1], own[1])))
    far.append(swap(other[2], "xl"))
    own.append(z_step(after(own[2], other[1])))
    cross.append(z_step(after(cross[1], own[2])))
    other.append(z_step(after(other[2], cross[1])))
    far.append(swap(other[3], "xl"))
    own.append(z_step(after(own[3], other[2], far[1])))
    cross.append(z_step(after(cross[2], own[3])))
    cross.append(z_step(after(cross[3], far[2])))

    total_own, total_other = contract(
        weights,
        [
            [None, *mine, (1, own[1], after(cross[1], own[3], other[3], cross[3]))],
            [None, (1, other[1], far[1])],
        ],
        f"{name}_1",
    )
    last_other = after(other[3], own[4], cross[4], total_own)
    total_own, total_other = contract(
        weights,
        [
            [total_own, (2, own[2], cross[2])],
            [total_other, (2, other[2], far[2]), (3, last_other, far[3])],
        ],
        f"{name}_2",
    )
    mine = []
    both = swap(total_other, "core")
    mine += [(s, own[s], cross[s]) for s in (3, 4)]
    return contract(
        weights,
        [[total_own, *mine]],
        f"{name}_last",
        finish=finish,
        extras=[both],
        outs=outs,
        smem=smem,
    )


def per_device(tokens, w_query, w_value, w_out, doc_lengths):
    rows = tokens.shape[0]
    heads = lax.axis_size(HEAD)

    joined, unit = gathered_product(
        tokens,
        [w_query, w_value],
        finish_units,
        [jax.ShapeDtypeStruct((rows, 2 * HD), BF16), jax.ShapeDtypeStruct((rows, HD), BF16)],
        [doc_lengths],
        "project",
    )
    unit_other = swap(unit, "core")
    from_y, from_x = swap(joined, "yl"), swap(joined, "xh")
    from_yx = swap(joined, "yl", "xh")
    parts = column_parts(w_out, heads)
    w_cols = lax.all_to_all(after(parts, joined), HEAD, 0, 0).reshape(heads * HD, HD)
    unit_other = after(unit_other, w_cols)

    own, other = attend(
        doc_lengths, [(unit, None, True), (unit_other, None, False)], [(0, joined)], "attend_own"
    )
    own, other = attend(
        doc_lengths,
        [(unit, own, False), (unit_other, other, False)],
        [(4, from_y), (2, from_x)],
        "attend_near",
    )
    (other,) = attend(
        doc_lengths, [(unit_other, other, False)], [(6, from_yx)], "attend_far_other", out_type=BF16
    )
    theirs = swap(other, "core")
    (own,) = attend(doc_lengths, [(unit, own, False)], [(6, from_yx)], "attend_far_own")
    attended = combine(doc_lengths, own, theirs, "combine")

    return gathered_product(
        attended,
        [w_cols],
        finish_out,
        [jax.ShapeDtypeStruct((rows, HD), BF16)],
        [],
        "output",
    )[0]


def solution(mesh):
    finer = Mesh(mesh.devices.reshape(2, 2, 2, 2, 2, 8), AXES)
    return jax.shard_map(
        per_device,
        mesh=finer,
        in_specs=(P(CTX, HEAD), P(None, HEAD), P(None, HEAD), P(HEAD, None), P()),
        out_specs=P(CTX, HEAD),
        check_vma=False,
    )
```

```python
import itertools
import math

import jax
import jax.numpy as jnp
from jax import lax
from jax.experimental import pallas as pl
from jax.experimental.pallas import tpu as pltpu
from jax.sharding import Mesh
from jax.sharding import PartitionSpec as P

HD = 128
ROWS = 1024
HEAD = ("xl", "z")
CTX = ("yh", "yl", "xh", "core")
AXES = CTX + HEAD
SCORE_BOUND = 24.0
SCALE = SCORE_BOUND * math.log2(math.e)
VMEM = pl.BlockSpec(memory_space=pltpu.VMEM)
SMEM = pl.BlockSpec(memory_space=pltpu.SMEM)
F32 = jnp.float32
BF16 = jnp.bfloat16


def hop(value, axes, target):
    places = list(itertools.product(*(range(lax.axis_size(a)) for a in axes)))
    number = {place: i for i, place in enumerate(places)}
    return lax.ppermute(value, axes, [(number[c], number[tuple(target(*c))]) for c in places])


def swap(value, *axes):
    return hop(value, axes, lambda *c: tuple(1 - i for i in c))


def z_step(value, way):
    depth = lax.axis_size("z")
    return hop(value, ("z",), lambda z: ((z - way) % depth,))


def params(mib):
    return pltpu.CompilerParams(vmem_limit_bytes=mib * 2**20)


def call(kernel, outs, smem_count, args, name, flops, limit=24):
    moved = sum(math.prod(a.shape) * a.dtype.itemsize for a in [*args, *outs])
    return pl.pallas_call(
        kernel,
        out_shape=outs,
        in_specs=[SMEM] * smem_count + [VMEM] * (len(args) - smem_count),
        out_specs=[VMEM] * len(outs),
        compiler_params=params(limit),
        cost_estimate=pl.CostEstimate(flops=flops, bytes_accessed=moved, transcendentals=0),
        name=name,
    )(*args)


def after(value, *others):
    return lax.optimization_barrier((value, *others))[0]


def valid_rows(doc_ref, mask):
    in_doc = (lax.axis_index("yl") * 2 + lax.axis_index("xh")) * 2 + lax.axis_index("core")
    return doc_ref[lax.axis_index("yh")] - (in_doc ^ mask) * ROWS


def contract(weights, jobs, name, finish=None, outs=None, smem=()):
    width = sum(w.shape[1] for w in weights)
    flat, plan = [], []
    for total, *terms in jobs:
        plan.append((total is not None, [t[0] for t in terms]))
        flat += ([total] if total is not None else []) + [b for t in terms for b in t[1:]]
    rows = jobs[0][1][1].shape[0]
    tile = 256
    if outs is None:
        outs = [jax.ShapeDtypeStruct((rows, width), F32)] * len(jobs)
    n_s, n_w, n_f = len(smem), len(weights), len(flat)
    depth = lax.axis_size("z")

    def kernel(*refs):
        w_refs = refs[n_s : n_s + n_w]
        b_refs = list(refs[n_s + n_w : n_s + n_w + n_f])
        o_refs = refs[n_s + n_w + n_f :]
        xl, z = lax.axis_index("xl"), lax.axis_index("z")
        taken = {}

        def weight(step):
            if step not in taken:
                z_at = (z + depth + step) % depth
                halves = []
                for side in (xl, 1 - xl):
                    first = pl.multiple_of((side * depth + z_at) * HD, HD)
                    halves.append(
                        jnp.concatenate([w[pl.ds(first, HD), :] for w in w_refs], axis=1)
                    )
                taken[step] = jnp.concatenate(halves, axis=0)
            return taken[step]

        for index, (has_total, steps) in enumerate(plan):
            total_ref = b_refs.pop(0) if has_total else None
            pairs = [(s, b_refs.pop(0), b_refs.pop(0)) for s in steps]
            for first in range(0, rows, tile):
                here = slice(first, first + tile)
                total = None if total_ref is None else total_ref[here, :]
                for s, one, two in pairs:
                    both = jnp.concatenate([one[here, :], two[here, :]], axis=1)
                    term = jnp.dot(both, weight(s), preferred_element_type=F32)
                    total = term if total is None else total + term
                if finish is None:
                    o_refs[index][here, :] = total.astype(o_refs[index].dtype)
                else:
                    finish(refs[:n_s], o_refs, total, first, tile)

    terms = sum(len(steps) for _, steps in plan)
    return call(
        kernel,
        outs,
        n_s,
        [*smem, *weights, *flat],
        name,
        2 * rows * 256 * width * terms,
    )


def finish_units(smem, outs, total, first, tile):
    here = slice(first, first + tile)
    proj = total[:, :HD]
    unit = proj * lax.rsqrt(jnp.sum(proj * proj, axis=-1, keepdims=True) + 1e-06)
    row = lax.broadcasted_iota(jnp.int32, (tile, HD), 0) + first
    value = jnp.where(row < valid_rows(smem[0], 0), total[:, HD:], 0.0).astype(BF16)
    unit = unit.astype(BF16)
    outs[0][here, :HD] = unit
    outs[0][here, HD:] = value
    outs[1][here, :] = unit


def finish_out(smem, outs, total, first, tile):
    here = slice(first, first + tile)
    outs[0][here, :] = total.astype(BF16)


def attend(doc_lengths, groups, blocks, name, out_type=F32, tile_q=512, tile_k=512):
    masks, blocks = zip(*blocks)
    n_b = len(blocks)
    flat, plan = [], []
    for queries, total, own in groups:
        plan.append((total is not None, own))
        flat += [queries] + ([total] if total is not None else [])
    rows = groups[0][0].shape[0]
    outs = [jax.ShapeDtypeStruct((rows, 2 * HD), out_type)] * len(groups)

    def kernel(*refs):
        limit = [valid_rows(refs[0], mask) for mask in masks]
        kv_refs = refs[1 : 1 + n_b]
        g_refs = list(refs[1 + n_b : 1 + n_b + len(flat)])
        o_refs = refs[1 + n_b + len(flat) :]
        for index, (has_total, own) in enumerate(plan):
            q_ref = g_refs.pop(0)
            t_ref = g_refs.pop(0) if has_total else None

            @pl.loop(0, rows // tile_q)
            def _(step):
                first = pl.multiple_of(step * tile_q, tile_q)
                here = pl.ds(first, tile_q)
                queries = q_ref[here, :]
                total = None if t_ref is None else t_ref[here, :]
                for b, kv in enumerate(kv_refs):
                    for start in range(0, kv.shape[0], tile_k):
                        keys = kv[start : start + tile_k, :HD]
                        values = kv[start : start + tile_k, HD:]
                        row = lax.broadcasted_iota(jnp.int32, (tile_k, HD), 0) + start
                        counted = jnp.where(row < limit[b], 1.0, 0.0).astype(BF16)
                        scores = lax.dot_general(
                            queries, keys, (((1,), (1,)), ((), ())), preferred_element_type=F32
                        )
                        weights = jnp.exp2(scores * SCALE - SCALE)
                        if own and b == 0:
                            q_at = lax.broadcasted_iota(jnp.int32, weights.shape, 0) + first
                            k_at = lax.broadcasted_iota(jnp.int32, weights.shape, 1) + start
                            weights = jnp.where(q_at == k_at, 0.0, weights)
                        term = jnp.dot(
                            weights.astype(BF16),
                            jnp.concatenate([values, counted], axis=1),
                            preferred_element_type=F32,
                        )
                        total = term if total is None else total + term
                o_refs[index][here, :] = total.astype(out_type)

    flops = len(groups) * n_b * 4 * rows * blocks[0].shape[0] * HD * 2
    return call(kernel, outs, 1, [doc_lengths, *blocks, *flat], name, flops)


def combine(doc_lengths, mine, theirs, name):
    rows = mine.shape[0]

    def kernel(doc_ref, a_ref, b_ref, o_ref):
        total = a_ref[...] + b_ref[...].astype(F32)
        row = lax.broadcasted_iota(jnp.int32, (rows, HD), 0)
        valid = row < valid_rows(doc_ref, 0)
        denom = jnp.where(valid, total[:, HD:], 1.0)
        o_ref[...] = jnp.where(valid, total[:, :HD] / denom, 0.0).astype(BF16)

    out = jax.ShapeDtypeStruct((rows, HD), BF16)
    return call(kernel, [out], 1, [doc_lengths, mine, theirs], name, rows * HD * 8)[0]


def column_parts(matrix, count):
    rows, width = matrix.shape[0], matrix.shape[1] // count

    def kernel(m_ref, o_ref):
        for i in range(count):
            o_ref[i] = m_ref[:, i * width : (i + 1) * width]

    out = jax.ShapeDtypeStruct((count, rows, width), matrix.dtype)
    return call(kernel, [out], 0, [matrix], "column_parts", 0)[0]


def gathered_product(block, weights, finish, outs, smem, name):
    assert lax.axis_size("z") == 8
    own, cross = {0: block}, {0: swap(block, "xl")}
    for s in (1, 2, 3):
        for way in (-1, 1):
            own[way * s] = z_step(own[way * (s - 1)], way)
            held = cross[way * (s - 1)]
            cross[way * s] = z_step(after(held, own[way]) if s == 1 else held, way)
    own[4], cross[4] = z_step(own[-3], -1), z_step(cross[3], 1)

    def terms(*places):
        return [(d, own[d], cross[d]) for d in places]

    own[0] = after(own[0], own[3], own[-3], cross[3], cross[-3])
    (total,) = contract(weights, [[None, *terms(0, 1, -1, 2, -2)]], f"{name}_near")
    return contract(
        weights,
        [[total, *terms(3, -3, 4)]],
        f"{name}_far",
        finish=finish,
        outs=outs,
        smem=smem,
    )


def per_device(tokens, w_query, w_value, w_out, doc_lengths):
    rows = tokens.shape[0]
    heads = lax.axis_size(HEAD)

    joined, unit = gathered_product(
        tokens,
        [w_query, w_value],
        finish_units,
        [jax.ShapeDtypeStruct((rows, 2 * HD), BF16), jax.ShapeDtypeStruct((rows, HD), BF16)],
        [doc_lengths],
        "project",
    )
    unit_other = swap(unit, "core")
    from_y, from_x = swap(joined, "yl"), swap(joined, "xh")
    from_yx = swap(joined, "yl", "xh")
    parts = column_parts(w_out, heads)

    own, other = attend(
        doc_lengths, [(unit, None, True), (unit_other, None, False)], [(0, joined)], "attend_own"
    )
    w_cols = lax.all_to_all(after(parts, own, from_y), HEAD, 0, 0).reshape(heads * HD, HD)
    own, other = attend(
        doc_lengths,
        [(unit, own, False), (unit_other, other, False)],
        [(4, from_y), (2, from_x)],
        "attend_near",
    )
    (other,) = attend(
        doc_lengths, [(unit_other, other, False)], [(6, from_yx)], "attend_far_other", out_type=BF16
    )
    theirs = swap(other, "core")
    (own,) = attend(doc_lengths, [(unit, own, False)], [(6, from_yx)], "attend_far_own")
    attended = combine(doc_lengths, after(own, w_cols), theirs, "combine")

    return gathered_product(
        attended,
        [w_cols],
        finish_out,
        [jax.ShapeDtypeStruct((rows, HD), BF16)],
        [],
        "output",
    )[0]


def solution(mesh):
    finer = Mesh(mesh.devices.reshape(2, 2, 2, 2, 2, 8), AXES)
    return jax.shard_map(
        per_device,
        mesh=finer,
        in_specs=(P(CTX, HEAD), P(None, HEAD), P(None, HEAD), P(HEAD, None), P()),
        out_specs=P(CTX, HEAD),
        check_vma=False,
    )
```

```python
import itertools
import math

import jax
import jax.numpy as jnp
from jax import lax
from jax.experimental import pallas as pl
from jax.experimental.pallas import tpu as pltpu
from jax.sharding import Mesh
from jax.sharding import PartitionSpec as P

HD = 128
ROWS = 1024
HEAD = ("xl", "z")
CTX = ("yh", "yl", "xh", "core")
AXES = CTX + HEAD
SCORE_BOUND = 24.0
SCALE = SCORE_BOUND * math.log2(math.e)
VMEM = pl.BlockSpec(memory_space=pltpu.VMEM)
SMEM = pl.BlockSpec(memory_space=pltpu.SMEM)
F32 = jnp.float32
BF16 = jnp.bfloat16


def hop(value, axes, target):
    places = list(itertools.product(*(range(lax.axis_size(a)) for a in axes)))
    number = {place: i for i, place in enumerate(places)}
    return lax.ppermute(value, axes, [(number[c], number[tuple(target(*c))]) for c in places])


def swap(value, *axes):
    return hop(value, axes, lambda *c: tuple(1 - i for i in c))


def z_step(value, way):
    depth = lax.axis_size("z")
    return hop(value, ("z",), lambda z: ((z - way) % depth,))


def params(mib):
    return pltpu.CompilerParams(vmem_limit_bytes=mib * 2**20)


def call(kernel, outs, smem_count, args, name, flops, limit=24):
    moved = sum(math.prod(a.shape) * a.dtype.itemsize for a in [*args, *outs])
    return pl.pallas_call(
        kernel,
        out_shape=outs,
        in_specs=[SMEM] * smem_count + [VMEM] * (len(args) - smem_count),
        out_specs=[VMEM] * len(outs),
        compiler_params=params(limit),
        cost_estimate=pl.CostEstimate(flops=flops, bytes_accessed=moved, transcendentals=0),
        name=name,
    )(*args)


def after(value, *others):
    return lax.optimization_barrier((value, *others))[0]


def valid_rows(doc_ref, mask):
    in_doc = (lax.axis_index("yl") * 2 + lax.axis_index("xh")) * 2 + lax.axis_index("core")
    return doc_ref[lax.axis_index("yh")] - (in_doc ^ mask) * ROWS


def contract(weights, jobs, name, finish=None, outs=None, smem=()):
    width = sum(w.shape[1] for w in weights)
    flat, plan = [], []
    for total, *terms in jobs:
        plan.append((total is not None, [t[0] for t in terms]))
        flat += ([total] if total is not None else []) + [b for t in terms for b in t[1:]]
    rows = jobs[0][1][1].shape[0]
    tile = 256
    if outs is None:
        outs = [jax.ShapeDtypeStruct((rows, width), F32)] * len(jobs)
    n_s, n_w, n_f = len(smem), len(weights), len(flat)
    depth = lax.axis_size("z")

    def kernel(*refs):
        w_refs = refs[n_s : n_s + n_w]
        b_refs = list(refs[n_s + n_w : n_s + n_w + n_f])
        o_refs = refs[n_s + n_w + n_f :]
        xl, z = lax.axis_index("xl"), lax.axis_index("z")
        taken = {}

        def weight(step):
            if step not in taken:
                z_at = (z + depth + step) % depth
                halves = []
                for side in (xl, 1 - xl):
                    first = pl.multiple_of((side * depth + z_at) * HD, HD)
                    halves.append(
                        jnp.concatenate([w[pl.ds(first, HD), :] for w in w_refs], axis=1)
                    )
                taken[step] = jnp.concatenate(halves, axis=0)
            return taken[step]

        for index, (has_total, steps) in enumerate(plan):
            total_ref = b_refs.pop(0) if has_total else None
            pairs = [(s, b_refs.pop(0), b_refs.pop(0)) for s in steps]
            for first in range(0, rows, tile):
                here = slice(first, first + tile)
                total = None if total_ref is None else total_ref[here, :]
                for s, one, two in pairs:
                    both = jnp.concatenate([one[here, :], two[here, :]], axis=1)
                    term = jnp.dot(both, weight(s), preferred_element_type=F32)
                    total = term if total is None else total + term
                if finish is None:
                    o_refs[index][here, :] = total.astype(o_refs[index].dtype)
                else:
                    finish(refs[:n_s], o_refs, total, first, tile)

    terms = sum(len(steps) for _, steps in plan)
    return call(
        kernel,
        outs,
        n_s,
        [*smem, *weights, *flat],
        name,
        2 * rows * 256 * width * terms,
    )


def finish_units(smem, outs, total, first, tile):
    here = slice(first, first + tile)
    proj = total[:, :HD]
    unit = proj * lax.rsqrt(jnp.sum(proj * proj, axis=-1, keepdims=True) + 1e-06)
    row = lax.broadcasted_iota(jnp.int32, (tile, HD), 0) + first
    value = jnp.where(row < valid_rows(smem[0], 0), total[:, HD:], 0.0).astype(BF16)
    unit = unit.astype(BF16)
    outs[0][here, :HD] = unit
    outs[0][here, HD:] = value
    outs[1][here, :] = unit


def finish_out(smem, outs, total, first, tile):
    here = slice(first, first + tile)
    outs[0][here, :] = total.astype(BF16)


def attend(doc_lengths, groups, blocks, name, out_type=F32, tile_q=1024, tile_k=512):
    masks, blocks = zip(*blocks)
    n_b = len(blocks)
    flat, plan = [], []
    for queries, total, own in groups:
        plan.append((total is not None, own))
        flat += [queries] + ([total] if total is not None else [])
    rows = groups[0][0].shape[0]
    outs = [jax.ShapeDtypeStruct((rows, 2 * HD), out_type)] * len(groups)

    def kernel(*refs):
        limit = [valid_rows(refs[0], mask) for mask in masks]
        kv_refs = refs[1 : 1 + n_b]
        g_refs = list(refs[1 + n_b : 1 + n_b + len(flat)])
        o_refs = refs[1 + n_b + len(flat) :]
        for index, (has_total, own) in enumerate(plan):
            q_ref = g_refs.pop(0)
            t_ref = g_refs.pop(0) if has_total else None

            @pl.loop(0, rows // tile_q)
            def _(step):
                first = pl.multiple_of(step * tile_q, tile_q)
                here = pl.ds(first, tile_q)
                queries = q_ref[here, :]
                total = None if t_ref is None else t_ref[here, :]
                for b, kv in enumerate(kv_refs):
                    for start in range(0, kv.shape[0], tile_k):
                        keys = kv[start : start + tile_k, :HD]
                        values = kv[start : start + tile_k, HD:]
                        row = lax.broadcasted_iota(jnp.int32, (tile_k, HD), 0) + start
                        counted = jnp.where(row < limit[b], 1.0, 0.0).astype(BF16)
                        scores = lax.dot_general(
                            queries, keys, (((1,), (1,)), ((), ())), preferred_element_type=F32
                        )
                        weights = jnp.exp2(scores * SCALE - SCALE)
                        if own and b == 0:
                            q_at = lax.broadcasted_iota(jnp.int32, weights.shape, 0) + first
                            k_at = lax.broadcasted_iota(jnp.int32, weights.shape, 1) + start
                            weights = jnp.where(q_at == k_at, 0.0, weights)
                        term = jnp.dot(
                            weights.astype(BF16),
                            jnp.concatenate([values, counted], axis=1),
                            preferred_element_type=F32,
                        )
                        total = term if total is None else total + term
                o_refs[index][here, :] = total.astype(out_type)

    flops = len(groups) * n_b * 4 * rows * blocks[0].shape[0] * HD * 2
    return call(kernel, outs, 1, [doc_lengths, *blocks, *flat], name, flops)


def combine(doc_lengths, mine, theirs, name):
    rows = mine.shape[0]

    def kernel(doc_ref, a_ref, b_ref, o_ref):
        total = a_ref[...] + b_ref[...].astype(F32)
        row = lax.broadcasted_iota(jnp.int32, (rows, HD), 0)
        valid = row < valid_rows(doc_ref, 0)
        denom = jnp.where(valid, total[:, HD:], 1.0)
        o_ref[...] = jnp.where(valid, total[:, :HD] / denom, 0.0).astype(BF16)

    out = jax.ShapeDtypeStruct((rows, HD), BF16)
    return call(kernel, [out], 1, [doc_lengths, mine, theirs], name, rows * HD * 8)[0]


def column_parts(matrix, count):
    rows, width = matrix.shape[0], matrix.shape[1] // count

    def kernel(m_ref, o_ref):
        for i in range(count):
            o_ref[i] = m_ref[:, i * width : (i + 1) * width]

    out = jax.ShapeDtypeStruct((count, rows, width), matrix.dtype)
    return call(kernel, [out], 0, [matrix], "column_parts", 0)[0]


def gathered_product(block, weights, finish, outs, smem, name):
    assert lax.axis_size("z") == 8
    own, cross = {0: block}, {0: swap(block, "xl")}

    def terms(*places):
        return [(d, own[d], cross[d]) for d in places]

    for s in (1, 2, 3):
        for way in (-1, 1):
            held = own[way * (s - 1)]
            own[way * s] = z_step(after(held, cross[way * (s - 2)]) if s > 2 else held, way)
        for way in (-1, 1):
            held = cross[way * (s - 1)]
            cross[way * s] = z_step(after(held, own[way * s]) if s > 1 else held, way)
    (total,) = contract(weights, [[None, *terms(0, 1, -1, 2, -2)]], f"{name}_near")
    own[4] = z_step(after(own[-3], total), -1)
    cross[4] = z_step(after(cross[3], total), 1)
    return contract(
        weights,
        [[total, *terms(3, -3, 4)]],
        f"{name}_far",
        finish=finish,
        outs=outs,
        smem=smem,
    )


def per_device(tokens, w_query, w_value, w_out, doc_lengths):
    rows = tokens.shape[0]
    heads = lax.axis_size(HEAD)

    joined, unit = gathered_product(
        tokens,
        [w_query, w_value],
        finish_units,
        [jax.ShapeDtypeStruct((rows, 2 * HD), BF16), jax.ShapeDtypeStruct((rows, HD), BF16)],
        [doc_lengths],
        "project",
    )
    unit_other = swap(unit, "core")
    from_y, from_x = swap(joined, "yl"), swap(joined, "xh")
    from_yx = swap(joined, "yl", "xh")
    parts = column_parts(w_out, heads)

    own, other = attend(
        doc_lengths, [(unit, None, True), (unit_other, None, False)], [(0, joined)], "attend_own"
    )
    w_cols = lax.all_to_all(after(parts, own, from_y), HEAD, 0, 0).reshape(heads * HD, HD)
    own, other = attend(
        doc_lengths,
        [(unit, own, False), (unit_other, other, False)],
        [(4, from_y), (2, from_x)],
        "attend_near",
    )
    (other,) = attend(
        doc_lengths, [(unit_other, other, False)], [(6, from_yx)], "attend_far_other", out_type=BF16
    )
    theirs = swap(other, "core")
    (own,) = attend(doc_lengths, [(unit, own, False)], [(6, from_yx)], "attend_far_own")
    attended = combine(doc_lengths, after(own, w_cols), theirs, "combine")

    return gathered_product(
        attended,
        [w_cols],
        finish_out,
        [jax.ShapeDtypeStruct((rows, HD), BF16)],
        [],
        "output",
    )[0]


def solution(mesh):
    finer = Mesh(mesh.devices.reshape(2, 2, 2, 2, 2, 8), AXES)
    return jax.shard_map(
        per_device,
        mesh=finer,
        in_specs=(P(CTX, HEAD), P(None, HEAD), P(None, HEAD), P(HEAD, None), P()),
        out_specs=P(CTX, HEAD),
        check_vma=False,
    )
```

```python
import itertools
import math

import jax
import jax.numpy as jnp
from jax import lax
from jax.experimental import pallas as pl
from jax.experimental.pallas import tpu as pltpu
from jax.sharding import Mesh
from jax.sharding import PartitionSpec as P

HD = 128
ROWS = 1024
HEAD = ("xl", "z")
CTX = ("yh", "yl", "xh", "core")
AXES = CTX + HEAD
SCORE_BOUND = 24.0
SCALE = SCORE_BOUND * math.log2(math.e)
VMEM = pl.BlockSpec(memory_space=pltpu.VMEM)
SMEM = pl.BlockSpec(memory_space=pltpu.SMEM)
F32 = jnp.float32
BF16 = jnp.bfloat16


def hop(value, axes, target):
    places = list(itertools.product(*(range(lax.axis_size(a)) for a in axes)))
    number = {place: i for i, place in enumerate(places)}
    return lax.ppermute(value, axes, [(number[c], number[tuple(target(*c))]) for c in places])


def swap(value, *axes):
    return hop(value, axes, lambda *c: tuple(1 - i for i in c))


def z_step(value, way):
    depth = lax.axis_size("z")
    return hop(value, ("z",), lambda z: ((z - way) % depth,))


def params(mib):
    return pltpu.CompilerParams(vmem_limit_bytes=mib * 2**20)


def call(kernel, outs, smem_count, args, name, flops, limit=24):
    moved = sum(math.prod(a.shape) * a.dtype.itemsize for a in [*args, *outs])
    return pl.pallas_call(
        kernel,
        out_shape=outs,
        in_specs=[SMEM] * smem_count + [VMEM] * (len(args) - smem_count),
        out_specs=[VMEM] * len(outs),
        compiler_params=params(limit),
        cost_estimate=pl.CostEstimate(flops=flops, bytes_accessed=moved, transcendentals=0),
        name=name,
    )(*args)


def after(value, *others):
    return lax.optimization_barrier((value, *others))[0]


def valid_rows(doc_ref, mask):
    in_doc = (lax.axis_index("yl") * 2 + lax.axis_index("xh")) * 2 + lax.axis_index("core")
    return doc_ref[lax.axis_index("yh")] - (in_doc ^ mask) * ROWS


def contract(weights, jobs, name, finish=None, outs=None, smem=()):
    width = sum(w.shape[1] for w in weights)
    flat, plan = [], []
    for total, *terms in jobs:
        plan.append((total is not None, [t[0] for t in terms]))
        flat += ([total] if total is not None else []) + [b for t in terms for b in t[1:]]
    rows = jobs[0][1][1].shape[0]
    tile = 256
    if outs is None:
        outs = [jax.ShapeDtypeStruct((rows, width), F32)] * len(jobs)
    n_s, n_w, n_f = len(smem), len(weights), len(flat)
    depth = lax.axis_size("z")

    def kernel(*refs):
        w_refs = refs[n_s : n_s + n_w]
        b_refs = list(refs[n_s + n_w : n_s + n_w + n_f])
        o_refs = refs[n_s + n_w + n_f :]
        xl, z = lax.axis_index("xl"), lax.axis_index("z")
        taken = {}

        def weight(step):
            if step not in taken:
                z_at = (z + depth + step) % depth
                halves = []
                for side in (xl, 1 - xl):
                    first = pl.multiple_of((side * depth + z_at) * HD, HD)
                    rows_here = [w[pl.ds(first, HD), :] for w in w_refs]
                    halves.append(jnp.concatenate(rows_here, axis=1))
                taken[step] = jnp.concatenate(halves, axis=0)
            return taken[step]

        for index, (has_total, steps) in enumerate(plan):
            total_ref = b_refs.pop(0) if has_total else None
            pairs = [(s, b_refs.pop(0), b_refs.pop(0)) for s in steps]
            for first in range(0, rows, tile):
                here = slice(first, first + tile)
                total = None if total_ref is None else total_ref[here, :]
                for s, one, two in pairs:
                    both = jnp.concatenate([one[here, :], two[here, :]], axis=1)
                    term = jnp.dot(both, weight(s), preferred_element_type=F32)
                    total = term if total is None else total + term
                if finish is None:
                    o_refs[index][here, :] = total.astype(o_refs[index].dtype)
                else:
                    finish(refs[:n_s], o_refs, total, first, tile)

    terms = sum(len(steps) for _, steps in plan)
    return call(
        kernel,
        outs,
        n_s,
        [*smem, *weights, *flat],
        name,
        2 * rows * 256 * width * terms,
    )


def finish_units(smem, outs, total, first, tile):
    here = slice(first, first + tile)
    row = lax.broadcasted_iota(jnp.int32, (tile, HD), 0) + first + lax.axis_index("xl") * (ROWS // 2)
    valid = row < valid_rows(smem[0], 0)
    for out, start in zip(outs, (0, 2 * HD)):
        proj = total[:, start : start + HD]
        unit = proj * lax.rsqrt(jnp.sum(proj * proj, axis=-1, keepdims=True) + 1e-06)
        value = jnp.where(valid, total[:, start + HD : start + 2 * HD], 0.0)
        out[here, :HD] = unit.astype(BF16)
        out[here, HD:] = value.astype(BF16)


def finish_out(smem, outs, total, first, tile):
    here = slice(first, first + tile)
    outs[0][here, :] = total[:, :HD].astype(BF16)
    outs[1][here, :] = total[:, HD:].astype(BF16)


def split_rows(block, name):
    half = block.shape[0] // 2

    def kernel(b_ref, mine_ref, theirs_ref):
        side = lax.axis_index("xl")
        mine_ref[...] = b_ref[pl.ds(pl.multiple_of(side * half, half), half), :]
        theirs_ref[...] = b_ref[pl.ds(pl.multiple_of((1 - side) * half, half), half), :]

    out = jax.ShapeDtypeStruct((half, block.shape[1]), block.dtype)
    return call(kernel, [out, out], 0, [block], name, 0)


def join_rows(mine, theirs, name, lead=False):
    half, width = mine.shape

    def kernel(m_ref, t_ref, o_ref, *lead_ref):
        side = lax.axis_index("xl")
        for ref, at in ((m_ref, side), (t_ref, 1 - side)):
            here = pl.ds(pl.multiple_of(at * half, half), half)
            o_ref[here, :] = ref[...]
            for l_ref in lead_ref:
                l_ref[here, :] = ref[:, :HD]

    outs = [jax.ShapeDtypeStruct((2 * half, width), mine.dtype)]
    if lead:
        outs.append(jax.ShapeDtypeStruct((2 * half, HD), mine.dtype))
    return call(kernel, outs, 0, [mine, theirs], name, 0)


def attend(doc_lengths, groups, blocks, name, out_type=F32, tile_q=1024, tile_k=512):
    masks, blocks = zip(*blocks)
    n_b = len(blocks)
    flat, plan = [], []
    for queries, total, own in groups:
        plan.append((total is not None, own))
        flat += [queries] + ([total] if total is not None else [])
    rows = groups[0][0].shape[0]
    outs = [jax.ShapeDtypeStruct((rows, 2 * HD), out_type)] * len(groups)

    def kernel(*refs):
        limit = [valid_rows(refs[0], mask) for mask in masks]
        kv_refs = refs[1 : 1 + n_b]
        g_refs = list(refs[1 + n_b : 1 + n_b + len(flat)])
        o_refs = refs[1 + n_b + len(flat) :]
        for index, (has_total, own) in enumerate(plan):
            q_ref = g_refs.pop(0)
            t_ref = g_refs.pop(0) if has_total else None

            @pl.loop(0, rows // tile_q)
            def _(step):
                first = pl.multiple_of(step * tile_q, tile_q)
                here = pl.ds(first, tile_q)
                queries = q_ref[here, :]
                total = None if t_ref is None else t_ref[here, :]
                for b, kv in enumerate(kv_refs):
                    for start in range(0, kv.shape[0], tile_k):
                        keys = kv[start : start + tile_k, :HD]
                        values = kv[start : start + tile_k, HD:]
                        row = lax.broadcasted_iota(jnp.int32, (tile_k, HD), 0) + start
                        counted = jnp.where(row < limit[b], 1.0, 0.0).astype(BF16)
                        scores = lax.dot_general(
                            queries, keys, (((1,), (1,)), ((), ())), preferred_element_type=F32
                        )
                        weights = jnp.exp2(scores * SCALE - SCALE)
                        if own and b == 0:
                            q_at = lax.broadcasted_iota(jnp.int32, weights.shape, 0) + first
                            k_at = lax.broadcasted_iota(jnp.int32, weights.shape, 1) + start
                            weights = jnp.where(q_at == k_at, 0.0, weights)
                        term = jnp.dot(
                            weights.astype(BF16),
                            jnp.concatenate([values, counted], axis=1),
                            preferred_element_type=F32,
                        )
                        total = term if total is None else total + term
                o_refs[index][here, :] = total.astype(out_type)

    flops = len(groups) * n_b * 4 * rows * blocks[0].shape[0] * HD * 2
    return call(kernel, outs, 1, [doc_lengths, *blocks, *flat], name, flops)


def combine(doc_lengths, mine, theirs, name):
    rows = mine.shape[0]

    def kernel(doc_ref, a_ref, b_ref, o_ref):
        total = a_ref[...] + b_ref[...].astype(F32)
        row = lax.broadcasted_iota(jnp.int32, (rows, HD), 0)
        valid = row < valid_rows(doc_ref, 0)
        denom = jnp.where(valid, total[:, HD:], 1.0)
        o_ref[...] = jnp.where(valid, total[:, :HD] / denom, 0.0).astype(BF16)

    out = jax.ShapeDtypeStruct((rows, HD), BF16)
    return call(kernel, [out], 1, [doc_lengths, mine, theirs], name, rows * HD * 8)[0]


def column_parts(matrix, count):
    rows, width = matrix.shape[0], matrix.shape[1] // count

    def kernel(m_ref, o_ref):
        for i in range(count):
            o_ref[i] = m_ref[:, i * width : (i + 1) * width]

    out = jax.ShapeDtypeStruct((count, rows, width), matrix.dtype)
    return call(kernel, [out], 0, [matrix], "column_parts", 0)[0]


def gathered_product(block, weights, more, finish, outs, smem, name):
    assert lax.axis_size("z") == 8
    mine, theirs = split_rows(block, f"{name}_split")
    own, cross = {0: mine}, {0: swap(theirs, "xl")}
    for s in (1, 2, 3):
        for way in (-1, 1):
            own[way * s] = z_step(own[way * (s - 1)], way)
            held = cross[way * (s - 1)]
            cross[way * s] = z_step(after(held, own[way]) if s == 1 else held, way)
    own[4], cross[4] = z_step(own[-3], -1), z_step(cross[3], 1)
    weights = [*weights, *more((cross[0],))]

    def terms(*places):
        return [(d, own[d], cross[d]) for d in places]

    own[0] = after(own[0], own[3], own[-3])
    (total,) = contract(
        weights, [[None, *terms(0, 1, -1, 2, -2)]], f"{name}_near"
    )
    return contract(
        weights,
        [[total, *terms(3, -3, 4)]],
        f"{name}_far",
        finish=finish,
        outs=outs,
        smem=smem,
    )


def per_device(tokens, w_query, w_value, w_out, doc_lengths):
    rows = tokens.shape[0]
    heads = lax.axis_size(HEAD)

    half = rows // 2

    def partner_weights(early):
        return swap(after(w_query, *early), "xl"), swap(after(w_value, *early), "xl")

    mine, theirs = gathered_product(
        tokens,
        [w_query, w_value],
        partner_weights,
        finish_units,
        [jax.ShapeDtypeStruct((half, 2 * HD), BF16)] * 2,
        [doc_lengths],
        "project",
    )
    joined, unit = join_rows(mine, swap(theirs, "xl"), "join_units", lead=True)
    unit_other = swap(unit, "core")
    from_y, from_x = swap(joined, "yl"), swap(joined, "xh")
    from_yx = swap(joined, "yl", "xh")
    parts = column_parts(w_out, heads)

    own, other = attend(
        doc_lengths, [(unit, None, True), (unit_other, None, False)], [(0, joined)], "attend_own"
    )
    w_cols = lax.all_to_all(after(parts, own, from_y), HEAD, 0, 0).reshape(heads * HD, HD)
    own, other = attend(
        doc_lengths,
        [(unit, own, False), (unit_other, other, False)],
        [(4, from_y), (2, from_x)],
        "attend_near",
    )
    (other,) = attend(
        doc_lengths, [(unit_other, other, False)], [(6, from_yx)], "attend_far_other", out_type=BF16
    )
    theirs = swap(other, "core")
    (own,) = attend(doc_lengths, [(unit, own, False)], [(6, from_yx)], "attend_far_own")
    attended = combine(doc_lengths, after(own, w_cols), theirs, "combine")

    mine, theirs = gathered_product(
        attended,
        [w_cols],
        lambda early: [swap(after(w_cols, *early), "xl")],
        finish_out,
        [jax.ShapeDtypeStruct((half, HD), BF16)] * 2,
        [],
        "output",
    )
    return join_rows(mine, swap(theirs, "xl"), "join_out")[0]


def solution(mesh):
    finer = Mesh(mesh.devices.reshape(2, 2, 2, 2, 2, 8), AXES)
    return jax.shard_map(
        per_device,
        mesh=finer,
        in_specs=(P(CTX, HEAD), P(None, HEAD), P(None, HEAD), P(HEAD, None), P()),
        out_specs=P(CTX, HEAD),
        check_vma=False,
    )
```

```python
import itertools
import math

import jax
import jax.numpy as jnp
from jax import lax
from jax.experimental import pallas as pl
from jax.experimental.pallas import tpu as pltpu
from jax.sharding import Mesh
from jax.sharding import PartitionSpec as P

HD = 128
ROWS = 1024
HEAD = ("xl", "z")
CTX = ("yh", "yl", "xh", "core")
AXES = CTX + HEAD
SCORE_BOUND = 24.0
SCALE = SCORE_BOUND * math.log2(math.e)
VMEM = pl.BlockSpec(memory_space=pltpu.VMEM)
SMEM = pl.BlockSpec(memory_space=pltpu.SMEM)
F32 = jnp.float32
BF16 = jnp.bfloat16


def hop(value, axes, target):
    places = list(itertools.product(*(range(lax.axis_size(a)) for a in axes)))
    number = {place: i for i, place in enumerate(places)}
    return lax.ppermute(value, axes, [(number[c], number[tuple(target(*c))]) for c in places])


def swap(value, *axes):
    return hop(value, axes, lambda *c: tuple(1 - i for i in c))


def z_step(value, way):
    depth = lax.axis_size("z")
    return hop(value, ("z",), lambda z: ((z - way) % depth,))


def params(mib):
    return pltpu.CompilerParams(vmem_limit_bytes=mib * 2**20)


def call(kernel, outs, smem_count, args, name, flops, limit=24):
    moved = sum(math.prod(a.shape) * a.dtype.itemsize for a in [*args, *outs])
    return pl.pallas_call(
        kernel,
        out_shape=outs,
        in_specs=[SMEM] * smem_count + [VMEM] * (len(args) - smem_count),
        out_specs=[VMEM] * len(outs),
        compiler_params=params(limit),
        cost_estimate=pl.CostEstimate(flops=flops, bytes_accessed=moved, transcendentals=0),
        name=name,
    )(*args)


def after(value, *others):
    return lax.optimization_barrier((value, *others))[0]


def valid_rows(doc_ref, mask):
    in_doc = (lax.axis_index("yl") * 2 + lax.axis_index("xh")) * 2 + lax.axis_index("core")
    return doc_ref[lax.axis_index("yh")] - (in_doc ^ mask) * ROWS


def contract(weights, jobs, name, finish=None, outs=None, smem=()):
    width = sum(w.shape[1] for w in weights)
    flat, plan = [], []
    for total, *terms in jobs:
        plan.append((total is not None, [t[0] for t in terms]))
        flat += ([total] if total is not None else []) + [b for t in terms for b in t[1:]]
    rows = jobs[0][1][1].shape[0]
    tile = 256
    if outs is None:
        outs = [jax.ShapeDtypeStruct((rows, width), F32)] * len(jobs)
    n_s, n_w, n_f = len(smem), len(weights), len(flat)
    depth = lax.axis_size("z")

    def kernel(*refs):
        w_refs = refs[n_s : n_s + n_w]
        b_refs = list(refs[n_s + n_w : n_s + n_w + n_f])
        o_refs = refs[n_s + n_w + n_f :]
        xl, z = lax.axis_index("xl"), lax.axis_index("z")
        taken = {}

        def weight(step):
            if step not in taken:
                z_at = (z + depth + step) % depth
                halves = []
                for side in (xl, 1 - xl):
                    first = pl.multiple_of((side * depth + z_at) * HD, HD)
                    rows_here = [w[pl.ds(first, HD), :] for w in w_refs]
                    halves.append(jnp.concatenate(rows_here, axis=1))
                taken[step] = jnp.concatenate(halves, axis=0)
            return taken[step]

        for index, (has_total, steps) in enumerate(plan):
            total_ref = b_refs.pop(0) if has_total else None
            pairs = [(s, b_refs.pop(0), b_refs.pop(0)) for s in steps]
            for first in range(0, rows, tile):
                here = slice(first, first + tile)
                total = None if total_ref is None else total_ref[here, :]
                for s, one, two in pairs:
                    both = jnp.concatenate([one[here, :], two[here, :]], axis=1)
                    term = jnp.dot(both, weight(s), preferred_element_type=F32)
                    total = term if total is None else total + term
                if finish is None:
                    o_refs[index][here, :] = total.astype(o_refs[index].dtype)
                else:
                    finish(refs[:n_s], o_refs, total, first, tile)

    terms = sum(len(steps) for _, steps in plan)
    return call(
        kernel,
        outs,
        n_s,
        [*smem, *weights, *flat],
        name,
        2 * rows * 256 * width * terms,
    )


def finish_units(smem, outs, total, first, tile):
    here = slice(first, first + tile)
    row = lax.broadcasted_iota(jnp.int32, (tile, HD), 0) + first + lax.axis_index("xl") * (ROWS // 2)
    valid = row < valid_rows(smem[0], 0)
    for out, start in zip(outs, (0, 2 * HD)):
        proj = total[:, start : start + HD]
        unit = proj * lax.rsqrt(jnp.sum(proj * proj, axis=-1, keepdims=True) + 1e-06)
        value = jnp.where(valid, total[:, start + HD : start + 2 * HD], 0.0)
        out[here, :HD] = unit.astype(BF16)
        out[here, HD:] = value.astype(BF16)


def finish_out(smem, outs, total, first, tile):
    here = slice(first, first + tile)
    outs[0][here, :] = total[:, :HD].astype(BF16)
    outs[1][here, :] = total[:, HD:].astype(BF16)


def split_rows(block, name):
    half = block.shape[0] // 2

    def kernel(b_ref, mine_ref, theirs_ref):
        side = lax.axis_index("xl")
        mine_ref[...] = b_ref[pl.ds(pl.multiple_of(side * half, half), half), :]
        theirs_ref[...] = b_ref[pl.ds(pl.multiple_of((1 - side) * half, half), half), :]

    out = jax.ShapeDtypeStruct((half, block.shape[1]), block.dtype)
    return call(kernel, [out, out], 0, [block], name, 0)


def join_rows(mine, theirs, name, lead=False):
    half, width = mine.shape

    def kernel(m_ref, t_ref, o_ref, *lead_ref):
        side = lax.axis_index("xl")
        for ref, at in ((m_ref, side), (t_ref, 1 - side)):
            here = pl.ds(pl.multiple_of(at * half, half), half)
            o_ref[here, :] = ref[...]
            for l_ref in lead_ref:
                l_ref[here, :] = ref[:, :HD]

    outs = [jax.ShapeDtypeStruct((2 * half, width), mine.dtype)]
    if lead:
        outs.append(jax.ShapeDtypeStruct((2 * half, HD), mine.dtype))
    return call(kernel, outs, 0, [mine, theirs], name, 0)


def attend(doc_lengths, groups, blocks, name, out_type=F32, tile_q=1024, tile_k=512):
    masks, blocks = zip(*blocks)
    n_b = len(blocks)
    flat, plan = [], []
    for queries, total, own in groups:
        plan.append((total is not None, own))
        flat += [queries] + ([total] if total is not None else [])
    rows = groups[0][0].shape[0]
    outs = [jax.ShapeDtypeStruct((rows, 2 * HD), out_type)] * len(groups)

    def kernel(*refs):
        limit = [valid_rows(refs[0], mask) for mask in masks]
        kv_refs = refs[1 : 1 + n_b]
        g_refs = list(refs[1 + n_b : 1 + n_b + len(flat)])
        o_refs = refs[1 + n_b + len(flat) :]
        for index, (has_total, own) in enumerate(plan):
            q_ref = g_refs.pop(0)
            t_ref = g_refs.pop(0) if has_total else None

            @pl.loop(0, rows // tile_q)
            def _(step):
                first = pl.multiple_of(step * tile_q, tile_q)
                here = pl.ds(first, tile_q)
                queries = q_ref[here, :]
                total = None if t_ref is None else t_ref[here, :]
                for b, kv in enumerate(kv_refs):
                    for start in range(0, kv.shape[0], tile_k):
                        keys = kv[start : start + tile_k, :HD]
                        values = kv[start : start + tile_k, HD:]
                        row = lax.broadcasted_iota(jnp.int32, (tile_k, HD), 0) + start
                        counted = jnp.where(row < limit[b], 1.0, 0.0).astype(BF16)
                        scores = lax.dot_general(
                            queries, keys, (((1,), (1,)), ((), ())), preferred_element_type=F32
                        )
                        weights = jnp.exp2(scores * SCALE - SCALE)
                        if own and b == 0:
                            q_at = lax.broadcasted_iota(jnp.int32, weights.shape, 0) + first
                            k_at = lax.broadcasted_iota(jnp.int32, weights.shape, 1) + start
                            weights = jnp.where(q_at == k_at, 0.0, weights)
                        term = jnp.dot(
                            weights.astype(BF16),
                            jnp.concatenate([values, counted], axis=1),
                            preferred_element_type=F32,
                        )
                        total = term if total is None else total + term
                o_refs[index][here, :] = total.astype(out_type)

    flops = len(groups) * n_b * 4 * rows * blocks[0].shape[0] * HD * 2
    return call(kernel, outs, 1, [doc_lengths, *blocks, *flat], name, flops)


def combine(doc_lengths, mine, theirs, name):
    rows = mine.shape[0]

    def kernel(doc_ref, a_ref, b_ref, o_ref):
        total = a_ref[...] + b_ref[...].astype(F32)
        row = lax.broadcasted_iota(jnp.int32, (rows, HD), 0)
        valid = row < valid_rows(doc_ref, 0)
        denom = jnp.where(valid, total[:, HD:], 1.0)
        o_ref[...] = jnp.where(valid, total[:, :HD] / denom, 0.0).astype(BF16)

    out = jax.ShapeDtypeStruct((rows, HD), BF16)
    return call(kernel, [out], 1, [doc_lengths, mine, theirs], name, rows * HD * 8)[0]


def column_parts(matrix, count):
    rows, width = matrix.shape[0], matrix.shape[1] // count

    def kernel(m_ref, o_ref):
        for i in range(count):
            o_ref[i] = m_ref[:, i * width : (i + 1) * width]

    out = jax.ShapeDtypeStruct((count, rows, width), matrix.dtype)
    return call(kernel, [out], 0, [matrix], "column_parts", 0)[0]


def gathered_product(block, weights, more, finish, outs, smem, name):
    assert lax.axis_size("z") == 8
    mine, theirs = split_rows(block, f"{name}_split")
    own, cross = {0: mine}, {0: swap(theirs, "xl")}
    for s in (1, 2, 3):
        for way in (-1, 1):
            own[way * s] = z_step(own[way * (s - 1)], way)
            held = cross[way * (s - 1)]
            cross[way * s] = z_step(after(held, own[way]) if s == 1 else held, way)
    own[4], cross[4] = z_step(own[-3], -1), z_step(cross[3], 1)
    weights = [*weights, *more((cross[0],))]

    def terms(*places):
        return [(d, own[d], cross[d]) for d in places]

    own[0] = after(own[0], own[3], own[-3])
    (total,) = contract(
        weights, [[None, *terms(0, 1, -1, 2, -2)]], f"{name}_near"
    )
    return contract(
        weights,
        [[total, *terms(3, -3, 4)]],
        f"{name}_far",
        finish=finish,
        outs=outs,
        smem=smem,
    )


def per_device(tokens, w_query, w_value, w_out, doc_lengths):
    rows = tokens.shape[0]
    heads = lax.axis_size(HEAD)

    half = rows // 2

    def partner_weights(early):
        return swap(after(w_query, *early), "xl"), swap(after(w_value, *early), "xl")

    mine, theirs = gathered_product(
        tokens,
        [w_query, w_value],
        partner_weights,
        finish_units,
        [jax.ShapeDtypeStruct((half, 2 * HD), BF16)] * 2,
        [doc_lengths],
        "project",
    )
    parts = after(column_parts(w_out, heads), mine)
    w_cols = lax.all_to_all(parts, HEAD, 0, 0).reshape(heads * HD, HD)
    joined, unit = join_rows(mine, swap(theirs, "xl"), "join_units", lead=True)
    unit_other = after(swap(unit, "core"), w_cols)
    from_y, from_x = swap(joined, "yl"), swap(joined, "xh")
    from_yx = swap(joined, "yl", "xh")

    own, other = attend(
        doc_lengths, [(unit, None, True), (unit_other, None, False)], [(0, joined)], "attend_own"
    )
    own, other = attend(
        doc_lengths,
        [(unit, own, False), (unit_other, other, False)],
        [(4, from_y), (2, from_x)],
        "attend_near",
    )
    (other,) = attend(
        doc_lengths, [(unit_other, other, False)], [(6, from_yx)], "attend_far_other", out_type=BF16
    )
    theirs = swap(other, "core")
    (own,) = attend(doc_lengths, [(unit, own, False)], [(6, from_yx)], "attend_far_own")
    attended = combine(doc_lengths, own, theirs, "combine")

    mine, theirs = gathered_product(
        attended,
        [w_cols],
        lambda early: [swap(after(w_cols, *early), "xl")],
        finish_out,
        [jax.ShapeDtypeStruct((half, HD), BF16)] * 2,
        [],
        "output",
    )
    return join_rows(mine, swap(theirs, "xl"), "join_out")[0]


def solution(mesh):
    finer = Mesh(mesh.devices.reshape(2, 2, 2, 2, 2, 8), AXES)
    return jax.shard_map(
        per_device,
        mesh=finer,
        in_specs=(P(CTX, HEAD), P(None, HEAD), P(None, HEAD), P(HEAD, None), P()),
        out_specs=P(CTX, HEAD),
        check_vma=False,
    )
```

```python
import itertools
import math

import jax
import jax.numpy as jnp
from jax import lax
from jax.experimental import pallas as pl
from jax.experimental.pallas import tpu as pltpu
from jax.sharding import Mesh
from jax.sharding import PartitionSpec as P

HD = 128
ROWS = 1024
HEAD = ("xl", "z")
CTX = ("yh", "yl", "xh", "core")
AXES = CTX + HEAD
SCORE_BOUND = 24.0
SCALE = SCORE_BOUND * math.log2(math.e)
VMEM = pl.BlockSpec(memory_space=pltpu.VMEM)
SMEM = pl.BlockSpec(memory_space=pltpu.SMEM)
F32 = jnp.float32
BF16 = jnp.bfloat16


def hop(value, axes, target):
    places = list(itertools.product(*(range(lax.axis_size(a)) for a in axes)))
    number = {place: i for i, place in enumerate(places)}
    return lax.ppermute(value, axes, [(number[c], number[tuple(target(*c))]) for c in places])


def swap(value, *axes):
    return hop(value, axes, lambda *c: tuple(1 - i for i in c))


def z_step(value, way):
    depth = lax.axis_size("z")
    return hop(value, ("z",), lambda z: ((z - way) % depth,))


def params(mib):
    return pltpu.CompilerParams(vmem_limit_bytes=mib * 2**20)


def call(kernel, outs, smem_count, args, name, flops, limit=24):
    moved = sum(math.prod(a.shape) * a.dtype.itemsize for a in [*args, *outs])
    return pl.pallas_call(
        kernel,
        out_shape=outs,
        in_specs=[SMEM] * smem_count + [VMEM] * (len(args) - smem_count),
        out_specs=[VMEM] * len(outs),
        compiler_params=params(limit),
        cost_estimate=pl.CostEstimate(flops=flops, bytes_accessed=moved, transcendentals=0),
        name=name,
    )(*args)


def after(value, *others):
    return lax.optimization_barrier((value, *others))[0]


def valid_rows(doc_ref, mask):
    in_doc = (lax.axis_index("yl") * 2 + lax.axis_index("xh")) * 2 + lax.axis_index("core")
    return doc_ref[lax.axis_index("yh")] - (in_doc ^ mask) * ROWS


def contract(weights, jobs, name, finish=None, outs=None, smem=()):
    width = sum(w.shape[1] for w in weights)
    flat, plan = [], []
    for total, *terms in jobs:
        plan.append((total is not None, [t[0] for t in terms]))
        flat += ([total] if total is not None else []) + [b for t in terms for b in t[1:]]
    rows = jobs[0][1][1].shape[0]
    tile = 256
    if outs is None:
        outs = [jax.ShapeDtypeStruct((rows, width), F32)] * len(jobs)
    n_s, n_w, n_f = len(smem), len(weights), len(flat)
    depth = lax.axis_size("z")

    def kernel(*refs):
        w_refs = refs[n_s : n_s + n_w]
        b_refs = list(refs[n_s + n_w : n_s + n_w + n_f])
        o_refs = refs[n_s + n_w + n_f :]
        xl, z = lax.axis_index("xl"), lax.axis_index("z")
        taken = {}

        def weight(step):
            if step not in taken:
                z_at = (z + depth + step) % depth
                halves = []
                for side in (xl, 1 - xl):
                    first = pl.multiple_of((side * depth + z_at) * HD, HD)
                    rows_here = [w[pl.ds(first, HD), :] for w in w_refs]
                    halves.append(jnp.concatenate(rows_here, axis=1))
                taken[step] = jnp.concatenate(halves, axis=0)
            return taken[step]

        for index, (has_total, steps) in enumerate(plan):
            total_ref = b_refs.pop(0) if has_total else None
            pairs = [(s, b_refs.pop(0), b_refs.pop(0)) for s in steps]
            for first in range(0, rows, tile):
                here = slice(first, first + tile)
                total = None if total_ref is None else total_ref[here, :]
                for s, one, two in pairs:
                    both = jnp.concatenate([one[here, :], two[here, :]], axis=1)
                    term = jnp.dot(both, weight(s), preferred_element_type=F32)
                    total = term if total is None else total + term
                if finish is None:
                    o_refs[index][here, :] = total.astype(o_refs[index].dtype)
                else:
                    finish(refs[:n_s], o_refs, total, first, tile)

    terms = sum(len(steps) for _, steps in plan)
    return call(
        kernel,
        outs,
        n_s,
        [*smem, *weights, *flat],
        name,
        2 * rows * 256 * width * terms,
    )


def finish_units(smem, outs, total, first, tile):
    here = slice(first, first + tile)
    row = lax.broadcasted_iota(jnp.int32, (tile, HD), 0) + first + lax.axis_index("xl") * (ROWS // 2)
    valid = row < valid_rows(smem[0], 0)
    for out, start in zip(outs, (0, 2 * HD)):
        proj = total[:, start : start + HD]
        unit = proj * lax.rsqrt(jnp.sum(proj * proj, axis=-1, keepdims=True) + 1e-06)
        value = jnp.where(valid, total[:, start + HD : start + 2 * HD], 0.0)
        out[here, :HD] = unit.astype(BF16)
        out[here, HD:] = value.astype(BF16)


def finish_out(smem, outs, total, first, tile):
    here = slice(first, first + tile)
    outs[0][here, :] = total[:, :HD].astype(BF16)
    outs[1][here, :] = total[:, HD:].astype(BF16)


def split_rows(block, name):
    half = block.shape[0] // 2

    def kernel(b_ref, mine_ref, theirs_ref):
        side = lax.axis_index("xl")
        mine_ref[...] = b_ref[pl.ds(pl.multiple_of(side * half, half), half), :]
        theirs_ref[...] = b_ref[pl.ds(pl.multiple_of((1 - side) * half, half), half), :]

    out = jax.ShapeDtypeStruct((half, block.shape[1]), block.dtype)
    return call(kernel, [out, out], 0, [block], name, 0)


def join_rows(mine, theirs, name, lead=False):
    half, width = mine.shape

    def kernel(m_ref, t_ref, o_ref, *lead_ref):
        side = lax.axis_index("xl")
        for ref, at in ((m_ref, side), (t_ref, 1 - side)):
            here = pl.ds(pl.multiple_of(at * half, half), half)
            o_ref[here, :] = ref[...]
            for l_ref in lead_ref:
                l_ref[here, :] = ref[:, :HD]

    outs = [jax.ShapeDtypeStruct((2 * half, width), mine.dtype)]
    if lead:
        outs.append(jax.ShapeDtypeStruct((2 * half, HD), mine.dtype))
    return call(kernel, outs, 0, [mine, theirs], name, 0)


def attend(doc_lengths, groups, blocks, name, out_type=F32, tile_q=512, tile_k=512):
    masks, blocks = zip(*blocks)
    n_b = len(blocks)
    flat, plan = [], []
    for queries, total, own in groups:
        plan.append((total is not None, own))
        flat += [queries] + ([total] if total is not None else [])
    rows = groups[0][0].shape[0]
    outs = [jax.ShapeDtypeStruct((rows, 2 * HD), out_type)] * len(groups)

    def kernel(*refs):
        limit = [valid_rows(refs[0], mask) for mask in masks]
        kv_refs = refs[1 : 1 + n_b]
        g_refs = list(refs[1 + n_b : 1 + n_b + len(flat)])
        o_refs = refs[1 + n_b + len(flat) :]
        for index, (has_total, own) in enumerate(plan):
            q_ref = g_refs.pop(0)
            t_ref = g_refs.pop(0) if has_total else None

            @pl.loop(0, rows // tile_q)
            def _(step):
                first = pl.multiple_of(step * tile_q, tile_q)
                here = pl.ds(first, tile_q)
                queries = q_ref[here, :]
                total = None if t_ref is None else t_ref[here, :]
                for b, kv in enumerate(kv_refs):
                    for start in range(0, kv.shape[0], tile_k):
                        keys = kv[start : start + tile_k, :HD]
                        values = kv[start : start + tile_k, HD:]
                        row = lax.broadcasted_iota(jnp.int32, (tile_k, HD), 0) + start
                        counted = jnp.where(row < limit[b], 1.0, 0.0).astype(BF16)
                        scores = lax.dot_general(
                            queries, keys, (((1,), (1,)), ((), ())), preferred_element_type=F32
                        )
                        weights = jnp.exp2(scores * SCALE - SCALE)
                        if own and b == 0:
                            q_at = lax.broadcasted_iota(jnp.int32, weights.shape, 0) + first
                            k_at = lax.broadcasted_iota(jnp.int32, weights.shape, 1) + start
                            weights = jnp.where(q_at == k_at, 0.0, weights)
                        term = jnp.dot(
                            weights.astype(BF16),
                            jnp.concatenate([values, counted], axis=1),
                            preferred_element_type=F32,
                        )
                        total = term if total is None else total + term
                o_refs[index][here, :] = total.astype(out_type)

    flops = len(groups) * n_b * 4 * rows * blocks[0].shape[0] * HD * 2
    return call(kernel, outs, 1, [doc_lengths, *blocks, *flat], name, flops)


def combine(doc_lengths, mine, theirs, name):
    rows = mine.shape[0]

    def kernel(doc_ref, a_ref, b_ref, o_ref):
        total = a_ref[...] + b_ref[...].astype(F32)
        row = lax.broadcasted_iota(jnp.int32, (rows, HD), 0)
        valid = row < valid_rows(doc_ref, 0)
        denom = jnp.where(valid, total[:, HD:], 1.0)
        o_ref[...] = jnp.where(valid, total[:, :HD] / denom, 0.0).astype(BF16)

    out = jax.ShapeDtypeStruct((rows, HD), BF16)
    return call(kernel, [out], 1, [doc_lengths, mine, theirs], name, rows * HD * 8)[0]


def column_parts(matrix, count):
    rows, width = matrix.shape[0], matrix.shape[1] // count

    def kernel(m_ref, o_ref):
        for i in range(count):
            o_ref[i] = m_ref[:, i * width : (i + 1) * width]

    out = jax.ShapeDtypeStruct((count, rows, width), matrix.dtype)
    return call(kernel, [out], 0, [matrix], "column_parts", 0)[0]


def gathered_product(block, weights, more, finish, outs, smem, name):
    assert lax.axis_size("z") == 8
    mine, theirs = split_rows(block, f"{name}_split")
    own, cross = {0: mine}, {0: swap(theirs, "xl")}
    for s in (1, 2, 3):
        for way in (-1, 1):
            own[way * s] = z_step(own[way * (s - 1)], way)
            held = cross[way * (s - 1)]
            cross[way * s] = z_step(after(held, own[way]) if s == 1 else held, way)
    own[4], cross[4] = z_step(own[-3], -1), z_step(cross[3], 1)
    weights = [*weights, *more((cross[0],))]

    def terms(*places):
        return [(d, own[d], cross[d]) for d in places]

    own[0] = after(own[0], own[3], own[-3])
    (total,) = contract(
        weights, [[None, *terms(0, 1, -1, 2, -2)]], f"{name}_near"
    )
    return contract(
        weights,
        [[total, *terms(3, -3, 4)]],
        f"{name}_far",
        finish=finish,
        outs=outs,
        smem=smem,
    )


def per_device(tokens, w_query, w_value, w_out, doc_lengths):
    rows = tokens.shape[0]
    heads = lax.axis_size(HEAD)

    half = rows // 2

    def partner_weights(early):
        return swap(after(w_query, *early), "xl"), swap(after(w_value, *early), "xl")

    mine, theirs = gathered_product(
        tokens,
        [w_query, w_value],
        partner_weights,
        finish_units,
        [jax.ShapeDtypeStruct((half, 2 * HD), BF16)] * 2,
        [doc_lengths],
        "project",
    )
    joined, unit = join_rows(mine, swap(theirs, "xl"), "join_units", lead=True)
    unit_other = swap(unit, "core")
    from_y, from_x = swap(joined, "yl"), swap(joined, "xh")
    from_yx = swap(joined, "yl", "xh")
    parts = column_parts(w_out, heads)

    own, other = attend(
        doc_lengths, [(unit, None, True), (unit_other, None, False)], [(0, joined)], "attend_own", tile_q=256
    )
    w_cols = lax.all_to_all(after(parts, own, from_y), HEAD, 0, 0).reshape(heads * HD, HD)
    own, other = attend(
        doc_lengths,
        [(unit, own, False), (unit_other, other, False)],
        [(4, from_y), (2, from_x)],
        "attend_near",
    )
    (other,) = attend(
        doc_lengths, [(unit_other, other, False)], [(6, from_yx)], "attend_far_other", out_type=BF16
    )
    theirs = swap(other, "core")
    (own,) = attend(doc_lengths, [(unit, own, False)], [(6, from_yx)], "attend_far_own")
    attended = combine(doc_lengths, after(own, w_cols), theirs, "combine")

    mine, theirs = gathered_product(
        attended,
        [w_cols],
        lambda early: [swap(after(w_cols, *early), "xl")],
        finish_out,
        [jax.ShapeDtypeStruct((half, HD), BF16)] * 2,
        [],
        "output",
    )
    return join_rows(mine, swap(theirs, "xl"), "join_out")[0]


def solution(mesh):
    finer = Mesh(mesh.devices.reshape(2, 2, 2, 2, 2, 8), AXES)
    return jax.shard_map(
        per_device,
        mesh=finer,
        in_specs=(P(CTX, HEAD), P(None, HEAD), P(None, HEAD), P(HEAD, None), P()),
        out_specs=P(CTX, HEAD),
        check_vma=False,
    )
```

```python
import itertools
import math

import jax
import jax.numpy as jnp
from jax import lax
from jax.experimental import pallas as pl
from jax.experimental.pallas import tpu as pltpu
from jax.sharding import Mesh
from jax.sharding import PartitionSpec as P

HD = 128
ROWS = 1024
HEAD = ("xl", "z")
CTX = ("yh", "yl", "xh", "core")
AXES = CTX + HEAD
SCORE_BOUND = 24.0
SCALE = SCORE_BOUND * math.log2(math.e)
VMEM = pl.BlockSpec(memory_space=pltpu.VMEM)
SMEM = pl.BlockSpec(memory_space=pltpu.SMEM)
F32 = jnp.float32
BF16 = jnp.bfloat16


def hop(value, axes, target):
    places = list(itertools.product(*(range(lax.axis_size(a)) for a in axes)))
    number = {place: i for i, place in enumerate(places)}
    return lax.ppermute(value, axes, [(number[c], number[tuple(target(*c))]) for c in places])


def swap(value, *axes):
    return hop(value, axes, lambda *c: tuple(1 - i for i in c))


def z_step(value, way):
    depth = lax.axis_size("z")
    return hop(value, ("z",), lambda z: ((z - way) % depth,))


def params(mib):
    return pltpu.CompilerParams(vmem_limit_bytes=mib * 2**20)


def call(kernel, outs, smem_count, args, name, flops, limit=24):
    moved = sum(math.prod(a.shape) * a.dtype.itemsize for a in [*args, *outs])
    return pl.pallas_call(
        kernel,
        out_shape=outs,
        in_specs=[SMEM] * smem_count + [VMEM] * (len(args) - smem_count),
        out_specs=[VMEM] * len(outs),
        compiler_params=params(limit),
        cost_estimate=pl.CostEstimate(flops=flops, bytes_accessed=moved, transcendentals=0),
        name=name,
    )(*args)


def after(value, *others):
    return lax.optimization_barrier((value, *others))[0]


def valid_rows(doc_ref, mask):
    in_doc = (lax.axis_index("yl") * 2 + lax.axis_index("xh")) * 2 + lax.axis_index("core")
    return doc_ref[lax.axis_index("yh")] - (in_doc ^ mask) * ROWS


def contract(weights, jobs, name, finish=None, outs=None, smem=()):
    width = sum(w.shape[1] for w in weights)
    flat, plan = [], []
    for total, *terms in jobs:
        plan.append((total is not None, [t[0] for t in terms]))
        flat += ([total] if total is not None else []) + [b for t in terms for b in t[1:]]
    rows = jobs[0][1][1].shape[0]
    tile = 256
    if outs is None:
        outs = [jax.ShapeDtypeStruct((rows, width), F32)] * len(jobs)
    n_s, n_w, n_f = len(smem), len(weights), len(flat)
    depth = lax.axis_size("z")

    def kernel(*refs):
        w_refs = refs[n_s : n_s + n_w]
        b_refs = list(refs[n_s + n_w : n_s + n_w + n_f])
        o_refs = refs[n_s + n_w + n_f :]
        xl, z = lax.axis_index("xl"), lax.axis_index("z")
        taken = {}

        def weight(step):
            if step not in taken:
                z_at = (z + depth + step) % depth
                halves = []
                for side in (xl, 1 - xl):
                    first = pl.multiple_of((side * depth + z_at) * HD, HD)
                    rows_here = [w[pl.ds(first, HD), :] for w in w_refs]
                    halves.append(jnp.concatenate(rows_here, axis=1))
                taken[step] = jnp.concatenate(halves, axis=0)
            return taken[step]

        for index, (has_total, steps) in enumerate(plan):
            total_ref = b_refs.pop(0) if has_total else None
            pairs = [(s, b_refs.pop(0), b_refs.pop(0)) for s in steps]
            for first in range(0, rows, tile):
                here = slice(first, first + tile)
                total = None if total_ref is None else total_ref[here, :]
                for s, one, two in pairs:
                    both = jnp.concatenate([one[here, :], two[here, :]], axis=1)
                    term = jnp.dot(both, weight(s), preferred_element_type=F32)
                    total = term if total is None else total + term
                if finish is None:
                    o_refs[index][here, :] = total.astype(o_refs[index].dtype)
                else:
                    finish(refs[:n_s], o_refs, total, first, tile)

    terms = sum(len(steps) for _, steps in plan)
    return call(
        kernel,
        outs,
        n_s,
        [*smem, *weights, *flat],
        name,
        2 * rows * 256 * width * terms,
    )


def finish_units(smem, outs, total, first, tile):
    here = slice(first, first + tile)
    row = lax.broadcasted_iota(jnp.int32, (tile, HD), 0) + first + lax.axis_index("xl") * (ROWS // 2)
    valid = row < valid_rows(smem[0], 0)
    for out, start in zip(outs, (0, 2 * HD)):
        proj = total[:, start : start + HD]
        unit = proj * lax.rsqrt(jnp.sum(proj * proj, axis=-1, keepdims=True) + 1e-06)
        value = jnp.where(valid, total[:, start + HD : start + 2 * HD], 0.0)
        out[here, :HD] = unit.astype(BF16)
        out[here, HD:] = value.astype(BF16)


def finish_out(smem, outs, total, first, tile):
    here = slice(first, first + tile)
    outs[0][here, :] = total[:, :HD].astype(BF16)
    outs[1][here, :] = total[:, HD:].astype(BF16)


def split_rows(block, name):
    half = block.shape[0] // 2

    def kernel(b_ref, mine_ref, theirs_ref):
        side = lax.axis_index("xl")
        mine_ref[...] = b_ref[pl.ds(pl.multiple_of(side * half, half), half), :]
        theirs_ref[...] = b_ref[pl.ds(pl.multiple_of((1 - side) * half, half), half), :]

    out = jax.ShapeDtypeStruct((half, block.shape[1]), block.dtype)
    return call(kernel, [out, out], 0, [block], name, 0)


def join_rows(mine, theirs, name, lead=False):
    half, width = mine.shape

    def kernel(m_ref, t_ref, o_ref, *lead_ref):
        side = lax.axis_index("xl")
        for ref, at in ((m_ref, side), (t_ref, 1 - side)):
            here = pl.ds(pl.multiple_of(at * half, half), half)
            o_ref[here, :] = ref[...]
            for l_ref in lead_ref:
                l_ref[here, :] = ref[:, :HD]

    outs = [jax.ShapeDtypeStruct((2 * half, width), mine.dtype)]
    if lead:
        outs.append(jax.ShapeDtypeStruct((2 * half, HD), mine.dtype))
    return call(kernel, outs, 0, [mine, theirs], name, 0)


def attend(doc_lengths, groups, blocks, name, out_type=F32, tile_q=512, tile_k=512):
    masks, blocks = zip(*blocks)
    n_b = len(blocks)
    flat, plan = [], []
    for queries, total, own in groups:
        plan.append((total is not None, own))
        flat += [queries] + ([total] if total is not None else [])
    rows = groups[0][0].shape[0]
    outs = [jax.ShapeDtypeStruct((rows, 2 * HD), out_type)] * len(groups)

    def kernel(*refs):
        limit = [valid_rows(refs[0], mask) for mask in masks]
        kv_refs = refs[1 : 1 + n_b]
        g_refs = list(refs[1 + n_b : 1 + n_b + len(flat)])
        o_refs = refs[1 + n_b + len(flat) :]
        for index, (has_total, own) in enumerate(plan):
            q_ref = g_refs.pop(0)
            t_ref = g_refs.pop(0) if has_total else None

            @pl.loop(0, rows // tile_q)
            def _(step):
                first = pl.multiple_of(step * tile_q, tile_q)
                here = pl.ds(first, tile_q)
                queries = q_ref[here, :]
                total = None if t_ref is None else t_ref[here, :]
                for b, kv in enumerate(kv_refs):
                    for start in range(0, kv.shape[0], tile_k):
                        keys = kv[start : start + tile_k, :HD]
                        values = kv[start : start + tile_k, HD:]
                        row = lax.broadcasted_iota(jnp.int32, (tile_k, HD), 0) + start
                        counted = jnp.where(row < limit[b], 1.0, 0.0).astype(BF16)
                        scores = lax.dot_general(
                            queries, keys, (((1,), (1,)), ((), ())), preferred_element_type=F32
                        )
                        weights = jnp.exp2(scores * SCALE - SCALE)
                        if own and b == 0:
                            q_at = lax.broadcasted_iota(jnp.int32, weights.shape, 0) + first
                            k_at = lax.broadcasted_iota(jnp.int32, weights.shape, 1) + start
                            weights = jnp.where(q_at == k_at, 0.0, weights)
                        term = jnp.dot(
                            weights.astype(BF16),
                            jnp.concatenate([values, counted], axis=1),
                            preferred_element_type=F32,
                        )
                        total = term if total is None else total + term
                o_refs[index][here, :] = total.astype(out_type)

    flops = len(groups) * n_b * 4 * rows * blocks[0].shape[0] * HD * 2
    return call(kernel, outs, 1, [doc_lengths, *blocks, *flat], name, flops)


def combine(doc_lengths, mine, theirs, name):
    rows = mine.shape[0]

    def kernel(doc_ref, a_ref, b_ref, o_ref):
        total = a_ref[...] + b_ref[...].astype(F32)
        row = lax.broadcasted_iota(jnp.int32, (rows, HD), 0)
        valid = row < valid_rows(doc_ref, 0)
        denom = jnp.where(valid, total[:, HD:], 1.0)
        o_ref[...] = jnp.where(valid, total[:, :HD] / denom, 0.0).astype(BF16)

    out = jax.ShapeDtypeStruct((rows, HD), BF16)
    return call(kernel, [out], 1, [doc_lengths, mine, theirs], name, rows * HD * 8)[0]


def column_parts(matrix, count):
    rows, width = matrix.shape[0], matrix.shape[1] // count

    def kernel(m_ref, o_ref):
        for i in range(count):
            o_ref[i] = m_ref[:, i * width : (i + 1) * width]

    out = jax.ShapeDtypeStruct((count, rows, width), matrix.dtype)
    return call(kernel, [out], 0, [matrix], "column_parts", 0)[0]


def gathered_product(block, weights, more, finish, outs, smem, name):
    assert lax.axis_size("z") == 8
    mine, theirs = split_rows(block, f"{name}_split")
    own, cross = {0: mine}, {0: swap(theirs, "xl")}
    for s in (1, 2, 3):
        for way in (-1, 1):
            own[way * s] = z_step(own[way * (s - 1)], way)
            held = cross[way * (s - 1)]
            cross[way * s] = z_step(after(held, own[way]) if s == 1 else held, way)
    own[4], cross[4] = z_step(own[-3], -1), z_step(cross[3], 1)
    weights = [*weights, *more((cross[0],))]

    def terms(*places):
        return [(d, own[d], cross[d]) for d in places]

    own[0] = after(own[0], own[3], own[-3])
    (total,) = contract(
        weights, [[None, *terms(0, 1, -1, 2, -2)]], f"{name}_near"
    )
    return contract(
        weights,
        [[total, *terms(3, -3, 4)]],
        f"{name}_far",
        finish=finish,
        outs=outs,
        smem=smem,
    )


def per_device(tokens, w_query, w_value, w_out, doc_lengths):
    rows = tokens.shape[0]
    heads = lax.axis_size(HEAD)

    half = rows // 2

    def partner_weights(early):
        return swap(after(w_query, *early), "xl"), swap(after(w_value, *early), "xl")

    mine, theirs = gathered_product(
        tokens,
        [w_query, w_value],
        partner_weights,
        finish_units,
        [jax.ShapeDtypeStruct((half, 2 * HD), BF16)] * 2,
        [doc_lengths],
        "project",
    )
    joined, unit = join_rows(mine, swap(theirs, "xl"), "join_units", lead=True)
    unit_other = swap(unit, "core")
    from_y, from_x = swap(joined, "yl"), swap(joined, "xh")
    from_yx = swap(joined, "yl", "xh")
    parts = column_parts(w_out, heads)

    own, other = attend(
        doc_lengths, [(unit, None, True), (unit_other, None, False)], [(0, joined)], "attend_own", tile_q=256
    )
    w_cols = lax.all_to_all(after(parts, own, from_y), HEAD, 0, 0).reshape(heads * HD, HD)
    own, other = attend(
        doc_lengths,
        [(unit, own, False), (unit_other, other, False)],
        [(4, from_y), (2, from_x)],
        "attend_near",
    )
    (other,) = attend(
        doc_lengths, [(unit_other, other, False)], [(6, from_yx)], "attend_far_other", out_type=BF16
    )
    theirs = swap(other, "core")
    (own,) = attend(doc_lengths, [(unit, own, False)], [(6, from_yx)], "attend_far_own")
    attended = combine(doc_lengths, own, theirs, "combine")

    mine, theirs = gathered_product(
        attended,
        [w_cols],
        lambda early: [swap(after(w_cols, *early), "xl")],
        finish_out,
        [jax.ShapeDtypeStruct((half, HD), BF16)] * 2,
        [],
        "output",
    )
    return join_rows(mine, swap(theirs, "xl"), "join_out")[0]


def solution(mesh):
    finer = Mesh(mesh.devices.reshape(2, 2, 2, 2, 2, 8), AXES)
    return jax.shard_map(
        per_device,
        mesh=finer,
        in_specs=(P(CTX, HEAD), P(None, HEAD), P(None, HEAD), P(HEAD, None), P()),
        out_specs=P(CTX, HEAD),
        check_vma=False,
    )
```
